256 devices in a mesh: row: 8 (over x, core), col: 32 (over y, z).
Axes of the slice: x: 4, y: 4, z: 8, core: 2. Of those that a mesh axis runs over, the one named last changes fastest.
Arguments:
- activations: bfloat16 [4096, 8192], P('col', 'row'), may hold values from -6 to 6
- out_grads: bfloat16 [4096, 22016], P('row', 'col'), may hold values from -48 to 48
- basis: float32 [8192, 512], P('row'), may hold values from -0.0625 to 0.0625
- row_moment: float32 [512], P('row'), may hold values from 40960 to 409600
- col_moment: float32 [22016], P('col'), may hold values from 4096 to 819200
Outputs:
- weight_update: float32 [8192, 22016], P('row', 'col')
- row_next: float32 [512], P('row')
- col_next: float32 [22016], P('col')
The draws below stay inside these ranges and needn't reach their ends.
All inputs are finite; a program needn't handle non-finite values.
Results may differ from the reference program's by a relative error of at most 0.0003.
Values may be sent and summed in bfloat16 or wider, within the bound.
A program may use at most 64 MiB of HBM per device.

```python
import math
import jax
import jax.numpy as jnp
from jax import lax

D = 8192
F = 22016
R = 512
TOKENS = 4096
N_COL = 32


def draw_out_grads(key, part):
    key = jax.random.fold_in(key, 7)
    noise_key, rough_key, token_key = jax.random.split(key, 3)
    columns = jnp.arange(F).astype(jnp.float32) / F
    ramp = jnp.exp(jnp.log(10.0) * columns)
    rough = jnp.exp(jax.random.uniform(rough_key, (F,), jnp.float32, jnp.log(0.5), jnp.log(2.0)))
    token_scale = jnp.exp(jax.random.uniform(token_key, (TOKENS, 1), jnp.float32, jnp.log(0.5), jnp.log(2.0)))
    base = jnp.clip(jax.random.normal(noise_key, (TOKENS, F), jnp.float32), -6.0, 6.0)
    values = base * token_scale * ramp[None, :] * rough[None, :]
    return jnp.clip(values, -48.0, 48.0).astype(jnp.bfloat16)


def levels(stream_key, dims, cuts, least, largest):
    def one(axis_at, shards_of):
        draws = jax.random.uniform(jax.random.fold_in(jax.random.fold_in(stream_key, 6), axis_at), (shards_of,), jnp.float32, least / len(cuts), largest / len(cuts))
        return jnp.repeat(jnp.exp(draws), dims[axis_at] // shards_of).reshape((-1,) + (1,) * (len(dims) - axis_at - 1))

    factor_of = one(*cuts[0])
    for cut in cuts[1:]:
        factor_of = factor_of * one(*cut)
    return factor_of


def bell_draw(key, shape, scale, most, pieces=(), kind=jnp.bfloat16):
    values = jax.random.normal(key, shape, jnp.float32) * scale
    if len(pieces) > 0:
        values = levels(key, shape, pieces, -0.22, 0.18) * values
    return jnp.clip(values, min=-most, max=most).astype(kind)


def setup_inputs(seed: int = 0) -> dict:
    key_of = jax.random.split(jax.random.key(seed), 6)
    activations = bell_draw(key_of[0], (TOKENS, D), 1.0, 6.0, ((0, 32), (1, 8)))
    out_grads = draw_out_grads(jax.random.fold_in(key_of[5], 71), 0)
    basis = bell_draw(key_of[2], (D, R), D ** -0.5, 0.0625, ((0, 8),), jnp.float32)
    row_moment = jnp.clip(jnp.exp(math.log(409600.0) - 2.3025851 * jax.random.uniform(key_of[3], (R,), jnp.float32) ** levels(key_of[3], (R,), ((0, 8),), -0.2, 0.2)), 40960.0, 409600.0)
    col_moment = jnp.clip(jnp.exp(math.log(819200.0) - 5.2983174 * jax.random.uniform(key_of[4], (F,), jnp.float32) ** levels(key_of[4], (F,), ((0, 32),), -0.2, 0.2)), 4096.0, 819200.0)
    return dict(activations=activations, out_grads=out_grads, basis=basis, row_moment=row_moment, col_moment=col_moment)


beta_two = 0.8
scale_alpha = 0.25
epsilon = 1e-30

def reference(activations, out_grads, basis, row_moment, col_moment):
    width = F // N_COL
    blocks = out_grads.reshape(TOKENS, N_COL, width).transpose(1, 0, 2)

    def project(block):
        gradient = lax.dot_general(activations, block, (((0,), (0,)), ((), ())), preferred_element_type=jnp.float32)
        return lax.dot_general(basis, gradient, (((0,), (0,)), ((), ())), precision=lax.Precision.HIGHEST)
    projected = lax.map(project, blocks).transpose(1, 0, 2).reshape(R, F)
    squares = projected * projected + epsilon
    row_next = beta_two * row_moment + (1.0 - beta_two) * lax.optimization_barrier(jnp.mean(squares, axis=1))
    col_next = beta_two * col_moment + (1.0 - beta_two) * lax.optimization_barrier(jnp.mean(squares, axis=0))
    second = row_next[:, None] * col_next[None, :] / jnp.mean(row_next)
    normalized = projected / jnp.sqrt(second)
    weight_update = scale_alpha * jnp.dot(basis, normalized, precision=lax.Precision.HIGHEST)
    return (weight_update, row_next, col_next)
```

```python
import jax
import jax.numpy as jnp
from jax import lax
from jax.experimental import pallas as pl
from jax.experimental.pallas import tpu as pltpu
from jax.sharding import PartitionSpec as P

F = 22016
R = 512
MESH = pl.DeviceIdType.MESH
f32 = jnp.float32
bf16 = jnp.bfloat16

beta_two = 0.8
scale_alpha = 0.25
epsilon = 1e-30

NX, NY, NZ = 4, 4, 8
ROWS = 2 * NX
COLS = NY * NZ
RB = R // ROWS
TB = 128
TG = 512
FB = F // COLS
LIFT = 2.0 ** 7.875


def split(v):
    high = v.astype(bf16)
    return high, (v - high.astype(f32)).astype(bf16)


def encode(u):
    top = jnp.maximum(jnp.max(jnp.abs(u), axis=0, keepdims=True), 1e-30)
    w = u * (LIFT / top)
    w = w * w
    w = w * w
    w = w * w
    w = w * w
    return jnp.where(u < 0, -w, w).astype(bf16), top * (1.0 / LIFT)


def decode(code, unit):
    t = code.astype(f32)
    m = jnp.exp2(jnp.log2(jnp.abs(t)) * 0.0625)
    m = jnp.where(t == 0, 0.0, m)
    return jnp.where(t < 0, -m, m) * unit


def kernel(act, grads, basis, rm, cm, w_out, rn_out, cn_out,
           a_v, b_v, g_v, sp, srecv, senc, sunit, sall, uall, shl, acc,
           penc, punit, rst, rsall, rnown, rnall, p_h, p_l, w_v,
           ld, s1s, s1r, bds, bdr, bus, bur, gs, gfs, gpr, gmr, g2r, gss, gsr,
           pds, pdr, pus, pur, sps, spr, sus, sur, rss, rsr, rns, rnr, wsem, ysem):
    row, col = lax.axis_index("row"), lax.axis_index("col")
    x, k = row // 2, row % 2
    y, z = col // NZ, col % NZ

    def at_x(o):
        return (lax.rem(x + o + NX, NX) * 2 + k, col)

    sibling = (x * 2 + 1 - k, col)

    def send(src, dst, ssem, rsem, dev):
        pltpu.make_async_remote_copy(src_ref=src, dst_ref=dst, send_sem=ssem, recv_sem=rsem,
                                     device_id=dev, device_id_type=MESH).start()

    def arrived(ref, sem):
        pltpu.make_async_copy(ref, ref, sem).wait()

    load_b = pltpu.make_async_copy(basis, b_v, ld.at[0])
    load_a = pltpu.make_async_copy(act, a_v, ld.at[1])
    load_g = pltpu.make_async_copy(grads, g_v.at[row], ld.at[2])
    load_b.start()
    load_a.start()
    load_g.start()

    barrier = pltpu.get_barrier_semaphore()
    for i in range(1, ROWS):
        pl.semaphore_signal(barrier, inc=1, device_id=(lax.rem(row + i, ROWS), col), device_id_type=MESH)
    for i in range(1, NZ):
        pl.semaphore_signal(barrier, inc=1, device_id=(row, y * NZ + lax.rem(z + i, NZ)), device_id_type=MESH)
    for i in range(1, NY):
        pl.semaphore_signal(barrier, inc=1, device_id=(row, lax.rem(y + i, NY) * NZ + z), device_id_type=MESH)

    load_b.wait()
    load_a.wait()
    b_h, b_l = split(b_v[...])
    a = a_v[...]
    part = jnp.dot(a, b_h, preferred_element_type=f32) + jnp.dot(a, b_l, preferred_element_type=f32)
    sp[...] = part.T.reshape(ROWS, RB, TB)
    load_g.wait()
    pl.semaphore_wait(barrier, ROWS + NZ + NY - 3)

    for i in range(1, ROWS):
        peer = lax.rem(row + i, ROWS)
        send(sp.at[peer], srecv.at[i], s1s.at[i], s1r.at[i], (peer, col))
    for i in range(1, NY):
        pl.semaphore_signal(ysem, inc=1, device_id=(row, lax.rem(y + i, NY) * NZ + z), device_id_type=MESH)

    H = TG // 2
    for h in range(2):
        lo, hi = pl.ds(h * H, H), pl.ds((1 - h) * H, H)
        send(g_v.at[row, lo], g_v.at[row, lo], gs.at[h], gpr.at[h], at_x(1))
        send(g_v.at[row, hi], g_v.at[row, hi], gs.at[2 + h], gmr.at[1 - h], at_x(-1))
    send(g_v.at[row], g_v.at[row], gss.at[0], gsr.at[0], sibling)

    total = sp[row]
    for i in range(1, ROWS):
        arrived(srecv.at[i], s1r.at[i])
        total = total + srecv[i]
    code, unit = encode(total)
    senc[...] = code
    sunit[...] = unit
    sall[col] = code
    uall[col] = unit
    pl.semaphore_wait(ysem, NY - 1)

    @pl.loop(1, COLS)
    def _(i):
        peer = lax.rem(col + i, COLS)
        send(senc, sall.at[col], bds.at[i], bdr.at[i], (row, peer))
        send(sunit, uall.at[col], bus.at[i], bur.at[i], (row, peer))

    before = lax.rem(x + NX - 1, NX) * 2 + k
    after = lax.rem(x + 1, NX) * 2 + k
    across = lax.rem(x + 2, NX) * 2 + k
    h0, h1 = pl.ds(0, H), pl.ds(H, H)
    arrived(g_v.at[before, h0], gpr.at[0])
    send(g_v.at[before, h0], g_v.at[before, h0], gfs.at[0], g2r.at[0], at_x(1))
    arrived(g_v.at[after, h1], gmr.at[1])
    send(g_v.at[after, h1], g_v.at[after, h1], gfs.at[1], g2r.at[1], at_x(-1))
    send(g_v.at[before, h0], g_v.at[before, h0], gss.at[1], gsr.at[1], sibling)
    send(g_v.at[after, h1], g_v.at[after, h1], gss.at[2], gsr.at[2], sibling)
    arrived(g_v.at[before, h1], gpr.at[1])
    send(g_v.at[before, h1], g_v.at[before, h1], gss.at[3], gsr.at[3], sibling)
    arrived(g_v.at[after, h0], gmr.at[0])
    send(g_v.at[after, h0], g_v.at[after, h0], gss.at[4], gsr.at[4], sibling)

    @pl.loop(1, COLS)
    def _(i):
        arrived(senc, bdr.at[i])
        arrived(sunit, bur.at[i])

    @pl.loop(0, ROWS)
    def _(r):
        for j in range(TG // TB):
            high, low = split(decode(sall[r * (TG // TB) + j], uall[r * (TG // TB) + j]))
            shl[r, 0:RB, j * TB:(j + 1) * TB] = high
            shl[r, RB:2 * RB, j * TB:(j + 1) * TB] = low

    def project(r):
        return jnp.dot(shl[r], g_v[r], preferred_element_type=f32)

    acc[...] = project(row)
    acc[...] += project(before)
    acc[...] += project(after)
    arrived(g_v.at[row], gsr.at[0])
    other = 1 - 2 * k
    acc[...] += project(row + other)
    arrived(g_v.at[before, h0], gsr.at[1])
    arrived(g_v.at[before, h0], gsr.at[3])
    acc[...] += project(before + other)
    arrived(g_v.at[before, h0], gsr.at[2])
    arrived(g_v.at[before, h0], gsr.at[4])
    acc[...] += project(after + other)
    arrived(g_v.at[across, h0], g2r.at[0])
    send(g_v.at[across, h0], g_v.at[across, h0], gss.at[5], gsr.at[5], sibling)
    arrived(g_v.at[across, h1], g2r.at[1])
    send(g_v.at[across, h1], g_v.at[across, h1], gss.at[6], gsr.at[6], sibling)
    acc[...] += project(across)
    arrived(g_v.at[across, h0], gsr.at[5])
    arrived(g_v.at[across, h1], gsr.at[6])
    acc[...] += project(across + other)

    mine = acc[0:RB] + acc[RB:2 * RB]
    code, unit = encode(mine)
    penc[row] = code
    punit[row] = unit
    for i in range(1, NX):
        send(penc.at[row], penc.at[row], pds.at[i], pdr.at[i], at_x(i))
        send(punit.at[row], punit.at[row], pus.at[i], pur.at[i], at_x(i))
    send(penc.at[row], penc.at[row], sps.at[0], spr.at[0], sibling)
    send(punit.at[row], punit.at[row], sus.at[0], sur.at[0], sibling)

    squares = mine * mine + epsilon
    none = jnp.zeros_like(squares)
    wide = jnp.where(k == 0, jnp.concatenate([squares, none], axis=0), jnp.concatenate([none, squares], axis=0))
    sums = lax.dot_general(jnp.ones((8, FB), f32), wide, (((1,), (1,)), ((), ())),
                           precision=lax.Precision.HIGHEST, preferred_element_type=f32)
    rst[...] = sums[0:1]
    rsall[col] = sums[0:1]

    @pl.loop(1, COLS)
    def _(i):
        send(rst, rsall.at[col], rss.at[i], rsr.at[i], (row, lax.rem(col + i, COLS)))

    @pl.loop(1, COLS)
    def _(i):
        arrived(rst, rsr.at[i])

    lane = lax.broadcasted_iota(jnp.int32, (1, 2 * RB), 1)
    old = jnp.concatenate([rm[...], rm[...]], axis=1)
    row_next = beta_two * old + (1.0 - beta_two) * (jnp.sum(rsall[...], axis=0) / F)
    rn_out[...] = jnp.where(k == 0, row_next[:, 0:RB], row_next[:, RB:2 * RB])
    row_next = jnp.where(lane // RB == k, row_next, 0.0)
    rnown[...] = row_next
    rnall[row] = row_next
    for i in range(1, ROWS):
        send(rnown, rnall.at[row], rns.at[i], rnr.at[i], (lax.rem(row + i, ROWS), col))

    for i in (1, 3, 2):
        piece = lax.rem(x + NX - i, NX) * 2 + k
        arrived(penc.at[piece], pdr.at[i])
        send(penc.at[piece], penc.at[piece], sps.at[i], spr.at[i], sibling)
        arrived(punit.at[piece], pur.at[i])
        send(punit.at[piece], punit.at[piece], sus.at[i], sur.at[i], sibling)
    for i in range(NX):
        arrived(penc.at[row], spr.at[i])
        arrived(punit.at[row], sur.at[i])

    col_sum = jnp.zeros((1, FB), f32)
    for r in range(ROWS):
        u = decode(penc[r], punit[r])
        col_sum = col_sum + jnp.sum(u * u + epsilon, axis=0, keepdims=True)
        high, low = split(u)
        p_h[r * RB:(r + 1) * RB, :] = high
        p_l[r * RB:(r + 1) * RB, :] = low
    col_next = beta_two * cm[...] + (1.0 - beta_two) * (col_sum / R)
    cn_out[...] = col_next

    for i in range(1, ROWS):
        arrived(rnown, rnr.at[i])
    rows = jnp.concatenate([rnall[2 * i] + rnall[2 * i + 1] for i in range(NX)], axis=1)
    by_row = 1.0 / jnp.sqrt(rows)
    row_mean = jnp.sum(rows, axis=1, keepdims=True) / R
    by_col = scale_alpha * jnp.sqrt(row_mean) / jnp.sqrt(col_next)
    M = 256
    for m in range(4):
        high, low = split(b_v[m * M:(m + 1) * M, :] * by_row)
        w = jnp.dot(high, p_h[...], preferred_element_type=f32)
        w += jnp.dot(high, p_l[...], preferred_element_type=f32)
        w += jnp.dot(low, p_h[...], preferred_element_type=f32)
        w_v[m * M:(m + 1) * M, :] = w * by_col
        pltpu.make_async_copy(w_v.at[pl.ds(m * M, M)], w_out.at[pl.ds(m * M, M)], wsem.at[m]).start()

    for i in range(1, ROWS):
        arrived(srecv.at[i], s1s.at[i])
        arrived(rnown, rns.at[i])

    @pl.loop(1, COLS)
    def _(i):
        arrived(senc, bds.at[i])
        arrived(sunit, bus.at[i])
        arrived(rst, rss.at[i])
    for i in range(4):
        arrived(g_v.at[row, h0], gs.at[i])
    for i in range(2):
        arrived(g_v.at[row, h0], gfs.at[i])
    arrived(g_v.at[row], gss.at[0])
    for i in range(1, 7):
        arrived(g_v.at[row, h0], gss.at[i])
    for i in range(NX):
        arrived(penc.at[row], sps.at[i])
        arrived(punit.at[row], sus.at[i])
    for i in range(1, NX):
        arrived(penc.at[row], pds.at[i])
        arrived(punit.at[row], pus.at[i])
    for m in range(4):
        pltpu.make_async_copy(w_v.at[pl.ds(m * M, M)], w_out.at[pl.ds(m * M, M)], wsem.at[m]).wait()


def per_device(activations, out_grads, basis, row_moment, col_moment):
    any_spec = pl.BlockSpec(memory_space=pl.ANY)
    vmem = pl.BlockSpec(memory_space=pltpu.VMEM)
    dma = pltpu.SemaphoreType.DMA
    w, rn, cn = pl.pallas_call(
        kernel,
        out_shape=(
            jax.ShapeDtypeStruct((1024, FB), f32),
            jax.ShapeDtypeStruct((1, RB), f32),
            jax.ShapeDtypeStruct((1, FB), f32),
        ),
        in_specs=[any_spec, any_spec, any_spec, vmem, vmem],
        out_specs=(any_spec, vmem, vmem),
        scratch_shapes=[
            pltpu.VMEM((TB, 1024), bf16),
            pltpu.VMEM((1024, R), f32),
            pltpu.VMEM((ROWS, TG, FB), bf16),
            pltpu.VMEM((ROWS, RB, TB), f32),
            pltpu.VMEM((ROWS, RB, TB), f32),
            pltpu.VMEM((RB, TB), bf16),
            pltpu.VMEM((1, TB), f32),
            pltpu.VMEM((COLS, RB, TB), bf16),
            pltpu.VMEM((COLS, 1, TB), f32),
            pltpu.VMEM((ROWS, 2 * RB, TG), bf16),
            pltpu.VMEM((2 * RB, FB), f32),
            pltpu.VMEM((ROWS, RB, FB), bf16),
            pltpu.VMEM((ROWS, 1, FB), f32),
            pltpu.VMEM((1, 2 * RB), f32),
            pltpu.VMEM((COLS, 1, 2 * RB), f32),
            pltpu.VMEM((1, 2 * RB), f32),
            pltpu.VMEM((ROWS, 1, 2 * RB), f32),
            pltpu.VMEM((R, FB), bf16),
            pltpu.VMEM((R, FB), bf16),
            pltpu.VMEM((1024, FB), f32),
            dma((3,)),
            dma((ROWS,)), dma((ROWS,)),
            dma((COLS,)), dma((COLS,)), dma((COLS,)), dma((COLS,)),
            dma((4,)), dma((2,)), dma((2,)), dma((2,)), dma((2,)), dma((7,)), dma((7,)),
            dma((NX,)), dma((NX,)), dma((NX,)), dma((NX,)),
            dma((NX,)), dma((NX,)), dma((NX,)), dma((NX,)),
            dma((COLS,)), dma((COLS,)),
            dma((ROWS,)), dma((ROWS,)),
            dma((4,)),
            pltpu.SemaphoreType.REGULAR,
        ],
        compiler_params=pltpu.CompilerParams(
            collective_id=0, has_side_effects=True, vmem_limit_bytes=48 * 2**20
        ),
    )(activations, out_grads, basis, row_moment.reshape(1, RB), col_moment.reshape(1, FB))
    return w, rn.reshape(RB), cn.reshape(FB)


def solution(mesh):
    in_specs = (P("col", "row"), P("row", "col"), P("row", None), P("row"), P("col"))
    out_specs = (P("row", "col"), P("row"), P("col"))
    return jax.shard_map(
        per_device, mesh=mesh, in_specs=in_specs, out_specs=out_specs, check_vma=False
    )
```

```python
import jax
import jax.numpy as jnp
from jax import lax
from jax.experimental import pallas as pl
from jax.experimental.pallas import tpu as pltpu
from jax.sharding import PartitionSpec as P

F = 22016
R = 512
MESH = pl.DeviceIdType.MESH
f32 = jnp.float32
bf16 = jnp.bfloat16

beta_two = 0.8
scale_alpha = 0.25
epsilon = 1e-30

NX, NY, NZ = 4, 4, 8
ROWS = 2 * NX
COLS = NY * NZ
RB = R // ROWS
RC = 2 * RB
TB = 128
TG = 512
DB = 1024
FB = F // COLS
FH = 352
LIFT = 2.0 ** 7.875


def split(v):
    high = v.astype(bf16)
    return high, (v - high.astype(f32)).astype(bf16)


def encode(u):
    top = jnp.maximum(jnp.max(jnp.abs(u), axis=0, keepdims=True), 1e-30)
    w = u * (LIFT / top)
    w = w * w
    w = w * w
    w = w * w
    w = w * w
    return jnp.where(u < 0, -w, w).astype(bf16), top * (1.0 / LIFT)


def decode(code, unit):
    t = code.astype(f32)
    m = jnp.exp2(jnp.log2(jnp.abs(t)) * 0.0625)
    m = jnp.where(t == 0, 0.0, m)
    return jnp.where(t < 0, -m, m) * unit


def exchange(act, grads, basis, rm, u_out, rows_out, rn_out, bh_out, bl_out,
             a_v, b_v, rm_v, g_own, g_v, sp, srecv, senc, sunit, sall, uall, shl, acc,
             penc, punit, rst, rsall, rnown, rnall,
             ld, s1s, s1r, bds, bdr, bus, bur, gps, gms, gfs, gpr, gmr, g2r, gss, gsr, sss, ssr,
             pds, pdr, pus, pur, sps, spr, sus, sur, rss, rsr, rns, rnr, ysem):
    row, col = lax.axis_index("row"), lax.axis_index("col")
    x, k = row // 2, row % 2
    y, z = col // NZ, col % NZ

    def at_x(o, core):
        return (lax.rem(x + o + NX, NX) * 2 + core, col)

    sibling = (x * 2 + 1 - k, col)

    def send(src, dst, ssem, rsem, dev):
        pltpu.make_async_remote_copy(src_ref=src, dst_ref=dst, send_sem=ssem, recv_sem=rsem,
                                     device_id=dev, device_id_type=MESH).start()

    def arrived(ref, sem):
        pltpu.make_async_copy(ref, ref, sem).wait()

    loads = [
        pltpu.make_async_copy(basis, b_v, ld.at[0]),
        pltpu.make_async_copy(act, a_v, ld.at[1]),
        pltpu.make_async_copy(grads.at[pl.ds(0, FH)], g_own.at[0], ld.at[2]),
        pltpu.make_async_copy(grads.at[pl.ds(FH, FB - FH)], g_own.at[1, pl.ds(0, FB - FH)], ld.at[3]),
        pltpu.make_async_copy(rm, rm_v, ld.at[4]),
    ]
    for load in loads:
        load.start()

    barrier = pltpu.get_barrier_semaphore()
    for i in range(1, ROWS):
        pl.semaphore_signal(barrier, inc=1, device_id=(lax.rem(row + i, ROWS), col), device_id_type=MESH)
    for i in range(1, NZ):
        pl.semaphore_signal(barrier, inc=1, device_id=(row, y * NZ + lax.rem(z + i, NZ)), device_id_type=MESH)
    for i in range(1, NY):
        pl.semaphore_signal(barrier, inc=1, device_id=(row, lax.rem(y + i, NY) * NZ + z), device_id_type=MESH)
    g_own[1, FB - FH:FH, :] = jnp.zeros((2 * FH - FB, TG), bf16)

    loads[0].wait()
    loads[1].wait()
    b_h, b_l = split(b_v[...])
    a = a_v[...]
    part = jnp.dot(a, b_h, preferred_element_type=f32) + jnp.dot(a, b_l, preferred_element_type=f32)
    sp[...] = part.T.reshape(ROWS, RB, TB)
    for load in loads[2:]:
        load.wait()
    pl.semaphore_wait(barrier, ROWS + NZ + NY - 3)

    for i in range(1, ROWS):
        peer = lax.rem(row + i, ROWS)
        send(sp.at[peer], srecv.at[i], s1s.at[i], s1r.at[i], (peer, col))
    for i in range(1, NY):
        pl.semaphore_signal(ysem, inc=1, device_id=(row, lax.rem(y + i, NY) * NZ + z), device_id_type=MESH)

    def send_up():
        for core in range(2):
            send(g_own.at[core], g_v.at[row], gps.at[core], gpr.at[k], at_x(1, core))

    def send_down():
        for core in range(2):
            send(g_own.at[core], g_v.at[row], gms.at[core], gmr.at[k], at_x(-1, core))

    send_up()
    send_down()
    send(g_own.at[1 - k], g_v.at[row], gss, gsr, sibling)

    total = sp[row]
    for i in range(1, ROWS):
        arrived(srecv.at[i], s1r.at[i])
        total = total + srecv[i]
    code, unit = encode(total)
    senc[...] = code
    sunit[...] = unit
    sall[k, col] = code
    uall[k, col] = unit
    pl.semaphore_wait(ysem, NY - 1)

    @pl.loop(1, COLS)
    def _(i):
        peer = lax.rem(col + i, COLS)
        send(senc, sall.at[k, col], bds.at[i], bdr.at[i], (row, peer))
        send(sunit, uall.at[k, col], bus.at[i], bur.at[i], (row, peer))

    before = lax.rem(x + NX - 1, NX) * 2
    after = lax.rem(x + 1, NX) * 2
    across = lax.rem(x + 2, NX) * 2
    arrived(g_v.at[before], gpr.at[0])
    send(g_v.at[before], g_v.at[before], gfs.at[0], g2r.at[0], at_x(1, k))
    arrived(g_v.at[after + 1], gmr.at[1])
    send(g_v.at[after + 1], g_v.at[after + 1], gfs.at[1], g2r.at[1], at_x(-1, k))

    turned_h, turned_l = split(b_v[...].T)
    bh_out[...] = turned_h
    bl_out[...] = turned_l

    @pl.loop(1, COLS)
    def _(i):
        arrived(senc, bdr.at[i])
        arrived(sunit, bur.at[i])
    send(sall.at[k], sall.at[k], sss.at[0], ssr.at[0], sibling)
    send(uall.at[k], uall.at[k], sss.at[1], ssr.at[1], sibling)
    arrived(sall.at[k], ssr.at[0])
    arrived(uall.at[k], ssr.at[1])

    @pl.loop(0, ROWS)
    def _(r):
        for j in range(TG // TB):
            b = r * (TG // TB) + j
            for core in range(2):
                high, low = split(decode(sall[core, b], uall[core, b]))
                shl[r, core * RB:(core + 1) * RB, j * TB:(j + 1) * TB] = high
                shl[r, RC + core * RB:RC + (core + 1) * RB, j * TB:(j + 1) * TB] = low

    def project(g, r):
        return lax.dot_general(g, shl[r], (((1,), (1,)), ((), ())), preferred_element_type=f32)

    acc[...] = project(g_own[k], row)
    arrived(g_v.at[row], gsr)
    acc[...] += project(g_v[x * 2 + 1 - k], x * 2 + 1 - k)
    acc[...] += project(g_v[before], before)
    arrived(g_v.at[before], gpr.at[1])
    acc[...] += project(g_v[before + 1], before + 1)
    acc[...] += project(g_v[after + 1], after + 1)
    arrived(g_v.at[after], gmr.at[0])
    acc[...] += project(g_v[after], after)
    arrived(g_v.at[across], g2r.at[0])
    acc[...] += project(g_v[across], across)
    arrived(g_v.at[across], g2r.at[1])
    acc[...] += project(g_v[across + 1], across + 1)

    mine = acc[:, 0:RC] + acc[:, RC:2 * RC]
    code, unit = encode(mine)
    penc[row] = code
    punit[row] = unit
    for i in range(1, NX):
        send(penc.at[row], penc.at[row], pds.at[i], pdr.at[i], at_x(i, k))
        send(punit.at[row], punit.at[row], pus.at[i], pur.at[i], at_x(i, k))
    send(penc.at[row], penc.at[row], sps.at[0], spr.at[0], sibling)
    send(punit.at[row], punit.at[row], sus.at[0], sur.at[0], sibling)

    count = jnp.where(k == 0, float(FH), float(FB - FH))
    sums = jnp.sum(mine * mine, axis=0, keepdims=True) + count * epsilon
    rst[...] = sums
    rsall[col] = sums

    @pl.loop(1, COLS)
    def _(i):
        send(rst, rsall.at[col], rss.at[i], rsr.at[i], (row, lax.rem(col + i, COLS)))

    @pl.loop(1, COLS)
    def _(i):
        arrived(rst, rsr.at[i])

    total = jnp.sum(rsall[...], axis=0)
    old = rm_v[...].reshape(1, RB)
    old = jnp.concatenate([old, old], axis=1)
    lane = lax.broadcasted_iota(jnp.int32, (1, RC), 1)
    mixed = (1.0 - beta_two) * (total / F) + jnp.where(lane // RB == k, beta_two * old, 0.0)
    rnown[...] = mixed
    rnall[row] = mixed
    for i in range(1, ROWS):
        send(rnown, rnall.at[row], rns.at[i], rnr.at[i], (lax.rem(row + i, ROWS), col))

    for i in (1, 3, 2):
        piece = lax.rem(x + NX - i, NX) * 2 + k
        arrived(penc.at[piece], pdr.at[i])
        send(penc.at[piece], penc.at[piece], sps.at[i], spr.at[i], sibling)
        arrived(punit.at[piece], pur.at[i])
        send(punit.at[piece], punit.at[piece], sus.at[i], sur.at[i], sibling)
    for i in range(NX):
        arrived(penc.at[row], spr.at[i])
        arrived(punit.at[row], sur.at[i])
    for r in range(ROWS):
        u_out[(r % 2) * FH:(r % 2 + 1) * FH, (r // 2) * RC:(r // 2 + 1) * RC] = decode(penc[r], punit[r])

    for i in range(1, ROWS):
        arrived(rnown, rnr.at[i])
    for i in range(NX):
        rows_out[:, i * RC:(i + 1) * RC] = rnall[2 * i] + rnall[2 * i + 1]
    chip = rnall[x * 2] + rnall[x * 2 + 1]
    rn_out[...] = jnp.where(k == 0, chip[:, 0:RB], chip[:, RB:RC])

    for i in range(1, ROWS):
        arrived(srecv.at[i], s1s.at[i])
        arrived(rnown, rns.at[i])

    @pl.loop(1, COLS)
    def _(i):
        arrived(senc, bds.at[i])
        arrived(sunit, bus.at[i])
        arrived(rst, rss.at[i])
    for i in range(2):
        arrived(g_v.at[row], gps.at[i])
        arrived(g_v.at[row], gms.at[i])
        arrived(g_v.at[row], gfs.at[i])
    arrived(g_v.at[row], gss)
    arrived(sall.at[k], sss.at[0])
    arrived(uall.at[k], sss.at[1])
    for i in range(NX):
        arrived(penc.at[row], sps.at[i])
        arrived(punit.at[row], sus.at[i])
    for i in range(1, NX):
        arrived(penc.at[row], pds.at[i])
        arrived(punit.at[row], pus.at[i])


MT = 344


def finish(u, rows, rn, bh, bl, cm, w_out, rn_out, cn_out, w_v, cm_v, cn_v, rn_v, sem):
    load = pltpu.make_async_copy(cm, cm_v, sem.at[2])
    load.start()
    rn_v[...] = rn[...].reshape(RB)
    put_rn = pltpu.make_async_copy(rn_v, rn_out, sem.at[3])
    put_rn.start()
    by_row = 1.0 / jnp.sqrt(rows[...])
    row_mean = jnp.sum(rows[...], axis=1, keepdims=True) / R
    top = scale_alpha * jnp.sqrt(row_mean)
    load.wait()
    old = jnp.broadcast_to(cm_v[...].reshape(1, FB), (128, FB)).T
    news = []
    puts = []
    for m in range(2):
        v = u[m * MT:(m + 1) * MT, :]
        col_sum = jnp.sum(v * v + epsilon, axis=1, keepdims=True)
        col_next = beta_two * old[m * MT:(m + 1) * MT] + (1.0 - beta_two) * (col_sum / R)
        news.append(col_next)
        by_col = top / jnp.sqrt(col_next[:, 0:1])
        high, low = split(v * by_row)
        w = jnp.dot(high, bh[...], preferred_element_type=f32)
        w += jnp.dot(low, bh[...], preferred_element_type=f32)
        w += jnp.dot(high, bl[...], preferred_element_type=f32)
        w_v[m * MT:(m + 1) * MT, :] = w * by_col
        put = pltpu.make_async_copy(w_v.at[pl.ds(m * MT, MT)], w_out.at[pl.ds(m * MT, MT)], sem.at[m])
        put.start()
        puts.append(put)
    cn_v[...] = jnp.concatenate(news, axis=0).T[0]
    put_cn = pltpu.make_async_copy(cn_v, cn_out, sem.at[4])
    put_cn.start()
    for put in puts + [put_rn, put_cn]:
        put.wait()


def per_device(activations, out_grads, basis, row_moment, col_moment):
    hbm = pl.BlockSpec(memory_space=pltpu.HBM)
    vmem = pl.BlockSpec(memory_space=pltpu.VMEM)
    dma = pltpu.SemaphoreType.DMA
    u, rows, rn, bh, bl = pl.pallas_call(
        exchange,
        out_shape=(
            jax.ShapeDtypeStruct((2 * FH, R), f32),
            jax.ShapeDtypeStruct((1, R), f32),
            jax.ShapeDtypeStruct((1, RB), f32),
            jax.ShapeDtypeStruct((R, DB), bf16),
            jax.ShapeDtypeStruct((R, DB), bf16),
        ),
        in_specs=[hbm] * 4,
        out_specs=(vmem,) * 5,
        scratch_shapes=[
            pltpu.VMEM((TB, DB), bf16),
            pltpu.VMEM((DB, R), f32),
            pltpu.VMEM((RB,), f32),
            pltpu.VMEM((2, FH, TG), bf16),
            pltpu.VMEM((ROWS, FH, TG), bf16),
            pltpu.VMEM((ROWS, RB, TB), f32),
            pltpu.VMEM((ROWS, RB, TB), f32),
            pltpu.VMEM((RB, TB), bf16),
            pltpu.VMEM((1, TB), f32),
            pltpu.VMEM((2, COLS, RB, TB), bf16),
            pltpu.VMEM((2, COLS, 1, TB), f32),
            pltpu.VMEM((ROWS, 2 * RC, TG), bf16),
            pltpu.VMEM((FH, 2 * RC), f32),
            pltpu.VMEM((ROWS, FH, RC), bf16),
            pltpu.VMEM((ROWS, 1, RC), f32),
            pltpu.VMEM((1, RC), f32),
            pltpu.VMEM((COLS, 1, RC), f32),
            pltpu.VMEM((1, RC), f32),
            pltpu.VMEM((ROWS, 1, RC), f32),
            dma((5,)),
            dma((ROWS,)), dma((ROWS,)),
            dma((COLS,)), dma((COLS,)), dma((COLS,)), dma((COLS,)),
            dma((2,)), dma((2,)), dma((2,)), dma((2,)), dma((2,)), dma((2,)), dma, dma, dma((2,)), dma((2,)),
            dma((NX,)), dma((NX,)), dma((NX,)), dma((NX,)),
            dma((NX,)), dma((NX,)), dma((NX,)), dma((NX,)),
            dma((COLS,)), dma((COLS,)),
            dma((ROWS,)), dma((ROWS,)),
            pltpu.SemaphoreType.REGULAR,
        ],
        compiler_params=pltpu.CompilerParams(
            collective_id=0, has_side_effects=True, vmem_limit_bytes=30 * 2**20
        ),
    )(*[pltpu.with_memory_space_constraint(v, pltpu.HBM) for v in (activations, out_grads.T, basis, row_moment)])
    w, rn, cn = pl.pallas_call(
        finish,
        out_shape=(
            jax.ShapeDtypeStruct((FB, DB), f32),
            jax.ShapeDtypeStruct((RB,), f32),
            jax.ShapeDtypeStruct((FB,), f32),
        ),
        in_specs=[vmem] * 5 + [hbm],
        out_specs=(hbm,) * 3,
        scratch_shapes=[
            pltpu.VMEM((FB, DB), f32),
            pltpu.VMEM((FB,), f32),
            pltpu.VMEM((FB,), f32),
            pltpu.VMEM((RB,), f32),
            dma((5,)),
        ],
        compiler_params=pltpu.CompilerParams(vmem_limit_bytes=30 * 2**20),
    )(u, rows, rn, bh, bl, col_moment)
    return w.T, rn, cn


def solution(mesh):
    in_specs = (P("col", "row"), P("row", "col"), P("row", None), P("row"), P("col"))
    out_specs = (P("row", "col"), P("row"), P("col"))
    return jax.shard_map(
        per_device, mesh=mesh, in_specs=in_specs, out_specs=out_specs, check_vma=False
    )
```

```python
import jax
import jax.numpy as jnp
from jax import lax
from jax.experimental import pallas as pl
from jax.experimental.pallas import tpu as pltpu
from jax.sharding import PartitionSpec as P

F = 22016
R = 512
MESH = pl.DeviceIdType.MESH
f32 = jnp.float32
bf16 = jnp.bfloat16

beta_two = 0.8
scale_alpha = 0.25
epsilon = 1e-30

NX, NY, NZ = 4, 4, 8
ROWS = 2 * NX
COLS = NY * NZ
RB = R // ROWS
RC = 2 * RB
TB = 128
TG = 512
DB = 1024
FB = F // COLS
FH = 352
FO = 2 * FH - FB
SB = RB // NY
LIFT = 2.0 ** 7.875


def split(v):
    high = v.astype(bf16)
    return high, (v - high.astype(f32)).astype(bf16)


def encode(u):
    top = jnp.maximum(jnp.max(jnp.abs(u), axis=0, keepdims=True), 1e-30)
    w = u * (LIFT / top)
    w = w * w
    w = w * w
    w = w * w
    w = w * w
    return jnp.where(u < 0, -w, w).astype(bf16), top * (1.0 / LIFT)


def decode(code, unit):
    t = code.astype(f32)
    m = jnp.exp2(jnp.log2(jnp.abs(t)) * 0.0625)
    m = jnp.where(t == 0, 0.0, m)
    return jnp.where(t < 0, -m, m) * unit


def exchange(act, grads, basis, rm, cm, u_out, rows_out, rn_out, cn_out, by_col_out, bh_out, bl_out,
             a_v, b_v, rm_v, cm_v, g_v, sp, su, srecv, urecv, frecv, furecv, senc, fenc, unit_own,
             sall, uall, fall, shl, shf, acc, fpenc, fpunit, fprecv, fpurecv,
             penc, punit, near_own, near_all, far_own, far_all,
             ld, s1s, s1r, u1s, u1r, f1s, f1r, fu1s, fu1r, bds, bdr, fds, fdr, fws, uzs, uzr, uys, uyr,
             g1s, g2s, g1r, g2r, gss, gsr, sss, ssr, fss, fsr, fps, fpr,
             pds, pdr, pus, pur, sps, spr, sus, sur, nes, ner, fas, far, ysem):
    row, col = lax.axis_index("row"), lax.axis_index("col")
    x, k = row // 2, row % 2
    y, z = col // NZ, col % NZ

    def at_x(o, core):
        return (lax.rem(x + o + NX, NX) * 2 + core, col)

    sibling = (x * 2 + 1 - k, col)
    opposite = lax.rem(x + 2, NX)
    here = y != opposite

    def send(src, dst, ssem, rsem, dev):
        pltpu.make_async_remote_copy(src_ref=src, dst_ref=dst, send_sem=ssem, recv_sem=rsem,
                                     device_id=dev, device_id_type=MESH).start()

    def arrived(ref, sem):
        pltpu.make_async_copy(ref, ref, sem).wait()

    def half(core):
        return grads.at[pl.ds(core * (FB - FH), FH)]

    loads = [
        pltpu.make_async_copy(basis, b_v, ld.at[0]),
        pltpu.make_async_copy(act, a_v, ld.at[1]),
        pltpu.make_async_copy(half(k), g_v.at[row], ld.at[2]),
        pltpu.make_async_copy(rm, rm_v, ld.at[3]),
        pltpu.make_async_copy(cm, cm_v, ld.at[4]),
    ]
    for load in loads:
        load.start()

    barrier = pltpu.get_barrier_semaphore()
    for i in range(1, ROWS):
        pl.semaphore_signal(barrier, inc=1, device_id=(lax.rem(row + i, ROWS), col), device_id_type=MESH)
    for i in range(1, NZ):
        pl.semaphore_signal(barrier, inc=1, device_id=(row, y * NZ + lax.rem(z + i, NZ)), device_id_type=MESH)
    for i in range(1, NY):
        pl.semaphore_signal(barrier, inc=1, device_id=(row, lax.rem(y + i, NY) * NZ + z), device_id_type=MESH)
    @pl.when(y != x)
    def _():
        for r in range(ROWS):
            pl.semaphore_signal(barrier, inc=1, device_id=(r, x * NZ + z), device_id_type=MESH)
    pl.semaphore_wait(barrier, ROWS + NZ + NY - 3 + 2 * (NY - 1))

    for i in range(1, NY):
        pl.semaphore_signal(ysem, inc=1, device_id=(row, lax.rem(y + i, NY) * NZ + z), device_id_type=MESH)

    loads[0].wait()
    loads[1].wait()
    b_h, b_l = split(b_v[...])
    a = a_v[...]
    part = jnp.dot(a, b_h, preferred_element_type=f32) + jnp.dot(a, b_l, preferred_element_type=f32)
    part = part.T
    for r in range(ROWS):
        code, unit = encode(part[r * RB:(r + 1) * RB])
        sp[r] = code
        su[r] = unit
    for i in range(1, ROWS):
        peer = lax.rem(row + i, ROWS)

        @pl.when(peer // 2 != lax.rem(y + 2, NY))
        def _():
            send(sp.at[peer], srecv.at[row], s1s.at[i], s1r.at[i], (peer, col))
            send(su.at[peer], urecv.at[row], u1s.at[i], u1r.at[i], (peer, col))
    over = lax.rem(y + 2, NY) * 2
    for core in range(2):
        for j in range(NY):
            @pl.when((y * 2 + core != row) | (y != j))
            def _():
                dev = (y * 2 + core, j * NZ + z)
                send(sp.at[over + core, pl.ds(j * SB, SB)], frecv.at[row], f1s.at[core * NY + j], f1r.at[row], dev)
                send(su.at[over + core], furecv.at[row], fu1s.at[core * NY + j], fu1r.at[row], dev)
    for core in range(2):
        send(half(core), g_v.at[row], g1s.at[core], g1r.at[k], at_x(1, core))
        send(half(core), g_v.at[row], g2s.at[core], g2r.at[k], at_x(-1, core))
    send(half(1 - k), g_v.at[row], gss, gsr, sibling)
    for load in loads[2:]:
        load.wait()

    pl.semaphore_wait(ysem, NY - 1)

    @pl.when(y == x)
    def _():
        frecv[row] = sp[opposite * 2 + k, pl.ds(pl.multiple_of(y * SB, SB), SB)]
        furecv[row] = su[opposite * 2 + k]
    for r in range(ROWS):
        @pl.when((y != x) | (row != r))
        def _():
            arrived(frecv.at[row], f1r.at[r])
            arrived(furecv.at[row], fu1r.at[r])
    total = decode(frecv[0], furecv[0])
    for r in range(1, ROWS):
        total = total + decode(frecv[r], furecv[r])
    code, unit = encode(total)
    fenc[...] = code
    unit_own[1] = unit
    fall[k, z, pl.ds(pl.multiple_of(y * SB, SB), SB)] = code
    unit_own[0] = unit

    @pl.when(here)
    def _():
        srecv[row] = sp[row]
        urecv[row] = su[row]
        for i in range(1, ROWS):
            arrived(srecv.at[row], s1r.at[i])
            arrived(urecv.at[row], u1r.at[i])
        total = decode(srecv[0], urecv[0])
        for r in range(1, ROWS):
            total = total + decode(srecv[r], urecv[r])
        code, unit = encode(total)
        senc[...] = code
        unit_own[0] = unit
        sall[k, col] = code
    uall[k, y, z] = unit_own[...]
    for j in range(1, NZ):
        send(unit_own, uall.at[k, y, z], uzs.at[j], uzr.at[j], (row, y * NZ + lax.rem(z + j, NZ)))

    for d in (1, 2, 3, 0):
        @pl.loop(0 if d else 1, NZ)
        def _(j):
            dev = (row, lax.rem(y + d, NY) * NZ + lax.rem(z + j, NZ))
            send(fenc, fall.at[k, z, pl.ds(pl.multiple_of(y * SB, SB), SB)], fds.at[d * NZ + j], fdr.at[d * NZ + j], dev)

    @pl.when(here)
    def _():
        for j in (2, 6, 1, 7, 0):
            for d in (1, 2, 3, 0):
                if j or d:
                    dev = (row, lax.rem(y + d, NY) * NZ + lax.rem(z + j, NZ))
                    send(senc, sall.at[k, col], bds.at[d * NZ + j], bdr.at[d * NZ + j], dev)

    before = lax.rem(x + NX - 1, NX) * 2
    after = lax.rem(x + 1, NX) * 2
    turned_h, turned_l = split(b_v[...].T)
    bh_out[...] = turned_h
    bl_out[...] = turned_l

    def project(g, sides):
        return lax.dot_general(g, sides, (((1,), (1,)), ((), ())), preferred_element_type=f32)

    for j in range(1, NZ):
        arrived(unit_own, uzr.at[j])
    for d in range(1, NY):
        send(uall.at[k, y], uall.at[k, y], uys.at[d], uyr.at[d], (row, lax.rem(y + d, NY) * NZ + z))

    def hand_on(d, source, j, sem):
        b = lax.rem(y + NY - d, NY) * NZ + lax.rem(z + source, NZ)
        dev = (row, y * NZ + lax.rem(z + j, NZ))
        send(sall.at[k, b], sall.at[k, b], fws.at[d * 4 + sem], bdr.at[d * NZ + lax.rem(NZ - source + j, NZ)], dev)

    for d in (1, 2, 3, 0):
        @pl.when(lax.rem(y + NY - d, NY) != opposite)
        def _():
            arrived(senc, bdr.at[d * NZ + 2])
            hand_on(d, NZ - 2, 1, 0)
            arrived(senc, bdr.at[d * NZ + 6])
            hand_on(d, 2, NZ - 1, 1)

            @pl.when(z % 2 == 0)
            def _():
                hand_on(d, NZ - 2, 2, 2)

            @pl.when(z % 2 == 1)
            def _():
                hand_on(d, 2, NZ - 2, 2)

    for d in (1, 2, 3, 0):
        @pl.loop(0 if d else 1, NZ)
        def _(j):
            arrived(fenc, fdr.at[d * NZ + j])
    send(fall.at[k], fall.at[k], fss.at[0], fsr.at[0], sibling)
    for d in range(1, NY):
        arrived(uall.at[k, y], uyr.at[d])
    send(uall.at[k], uall.at[k], fss.at[1], fsr.at[1], sibling)
    arrived(g_v.at[row], gsr)
    arrived(fall.at[k], fsr.at[0])
    arrived(uall.at[k], fsr.at[1])
    for b in range(NZ):
        r, at = b // 4, b % 4 * TB
        for core in range(2):
            units = jnp.concatenate([jnp.broadcast_to(uall[core, j, b, 1], (SB, TB)) for j in range(NY)], axis=0)
            high, low = split(decode(fall[core, b], units))
            shf[r, core * RB:(core + 1) * RB, at:at + TB] = high
            shf[r, RC + core * RB:RC + (core + 1) * RB, at:at + TB] = low
    acc[...] = project(g_v[x * 2], shf[0])
    acc[...] += project(g_v[x * 2 + 1], shf[1])
    code, unit = encode(acc[:, 0:RC] + acc[:, RC:2 * RC])
    fpenc[...] = code
    fpunit[...] = unit
    send(fpenc, fprecv, fps.at[0], fpr.at[0], at_x(2, k))
    send(fpunit, fpurecv, fps.at[1], fpr.at[1], at_x(2, k))

    def share(d):
        first = lax.rem(y + NY - d, NY)

        @pl.when(first != opposite)
        def _():
            for j in (0, 1, 7, 3, 4, 5):
                if j or d:
                    arrived(senc, bdr.at[d * NZ + j])
            some = pl.ds(first * NZ, NZ)
            send(sall.at[k, some], sall.at[k, some], sss.at[d], ssr.at[d], sibling)

    def unpack(d):
        first = lax.rem(y + NY - d, NY)

        @pl.when(first != opposite)
        def _():
            some = pl.ds(first * NZ, NZ)
            arrived(sall.at[k, some], ssr.at[d])
            for j in range(NZ):
                b = first * NZ + j
                r = first * 2 + j // 4
                at = j % 4 * TB
                for core in range(2):
                    high, low = split(decode(sall[core, b], uall[core, first, j, 0]))
                    shl[r, core * RB:(core + 1) * RB, at:at + TB] = high
                    shl[r, RC + core * RB:RC + (core + 1) * RB, at:at + TB] = low

    share(1)
    share(2)
    unpack(1)
    share(3)
    unpack(2)
    share(0)
    unpack(3)
    unpack(0)

    acc[...] = project(g_v[x * 2], shl[x * 2])
    acc[...] += project(g_v[x * 2 + 1], shl[x * 2 + 1])
    for i in range(2):
        arrived(g_v.at[row], g1r.at[i])
        acc[...] += project(g_v[before + i], shl[before + i])
    for i in range(2):
        arrived(g_v.at[row], g2r.at[i])
        acc[...] += project(g_v[after + i], shl[after + i])
    arrived(fprecv, fpr.at[0])
    arrived(fpurecv, fpr.at[1])

    mine = acc[:, 0:RC] + acc[:, RC:2 * RC] + decode(fprecv[...], fpurecv[...])
    own = lax.broadcasted_iota(jnp.int32, (FH, RC), 0) >= FO * k
    sums = jnp.sum(jnp.where(own, mine * mine + epsilon, 0.0), axis=0, keepdims=True)
    old = rm_v[...].reshape(1, RB)
    old = jnp.concatenate([old, old], axis=1)
    lane = lax.broadcasted_iota(jnp.int32, (1, RC), 1)
    joins = (lane // RB == k) & (col == 0)
    near = (1.0 - beta_two) * (sums / F) + jnp.where(joins, beta_two * old, 0.0)
    near_own[...] = near
    near_at = k * NZ + z
    near_all[near_at] = near

    @pl.loop(1, 2 * NZ)
    def _(i):
        to = lax.rem(near_at + i, 2 * NZ)
        send(near_own, near_all.at[near_at], nes.at[i], ner.at[i], (x * 2 + to // NZ, y * NZ + lax.rem(to, NZ)))

    code, unit = encode(mine)
    penc[row] = code
    punit[row] = unit
    for i in (2, 1, 3):
        send(penc.at[row], penc.at[row], pds.at[i], pdr.at[i], at_x(i, k))
        send(punit.at[row], punit.at[row], pus.at[i], pur.at[i], at_x(i, k))
    send(penc.at[row], penc.at[row], sps.at[0], spr.at[0], sibling)
    send(punit.at[row], punit.at[row], sus.at[0], sur.at[0], sibling)

    @pl.loop(1, 2 * NZ)
    def _(i):
        arrived(near_own, ner.at[i])

    mid = jnp.sum(near_all[...], axis=0)
    far_own[...] = mid
    far_at = y * NX + x
    far_all[far_at] = mid

    @pl.loop(1, NX * NY)
    def _(i):
        to = lax.rem(far_at + i, NX * NY)
        send(far_own, far_all.at[far_at], fas.at[i], far.at[i], (lax.rem(to, NX) * 2 + k, to // NX * NZ + z))

    for i in (1, 3, 2):
        piece = lax.rem(x + NX - i, NX) * 2 + k
        arrived(penc.at[piece], pdr.at[i])
        send(penc.at[piece], penc.at[piece], sps.at[i], spr.at[i], sibling)
        arrived(punit.at[piece], pur.at[i])
        send(punit.at[piece], punit.at[piece], sus.at[i], sur.at[i], sibling)
    for i in range(NX):
        arrived(penc.at[row], spr.at[i])
        arrived(punit.at[row], sur.at[i])
    col_sum = [jnp.zeros((FH, 1), f32), jnp.zeros((FB - FH, 1), f32)]
    for r in range(ROWS):
        c = r % 2
        u = decode(penc[r], punit[r])[FO * c:]
        u_out[c * FH:c * FH + FH - FO * c, (r // 2) * RC:(r // 2 + 1) * RC] = u
        col_sum[c] += jnp.sum(u * u + epsilon, axis=1, keepdims=True)
    old = jnp.broadcast_to(cm_v[...].reshape(1, FB), (128, FB)).T
    col_next = beta_two * old + (1.0 - beta_two) * (jnp.concatenate(col_sum, axis=0) / R)
    cn_out[...] = col_next.T[0]
    by_col_out[...] = 1.0 / jnp.sqrt(col_next)

    for i in range(1, ROWS):
        @pl.when(lax.rem(row + i, ROWS) // 2 != lax.rem(y + 2, NY))
        def _():
            arrived(srecv.at[row], s1s.at[i])
            arrived(urecv.at[row], u1s.at[i])
    for core in range(2):
        for j in range(NY):
            @pl.when((y * 2 + core != row) | (y != j))
            def _():
                arrived(frecv.at[row], f1s.at[core * NY + j])
                arrived(furecv.at[row], fu1s.at[core * NY + j])

    @pl.loop(1, COLS)
    def _(i):
        arrived(fenc, fds.at[i])

    @pl.when(here)
    def _():
        for d in range(NY):
            for j in (0, 1, 2, 6, 7):
                if j or d:
                    arrived(senc, bds.at[d * NZ + j])
    for j in range(1, NZ):
        arrived(unit_own, uzs.at[j])
    for d in range(1, NY):
        arrived(uall.at[k, y], uys.at[d])

    @pl.loop(1, 2 * NZ)
    def _(i):
        arrived(near_own, nes.at[i])
    for i in range(2):
        arrived(g_v.at[row], g1s.at[i])
        arrived(g_v.at[row], g2s.at[i])
    arrived(g_v.at[row], gss)
    arrived(fall.at[k], fss.at[0])
    arrived(uall.at[k], fss.at[1])
    arrived(fpenc, fps.at[0])
    arrived(fpunit, fps.at[1])
    for d in range(NY):
        @pl.when(lax.rem(y + NY - d, NY) != opposite)
        def _():
            arrived(sall.at[k, pl.ds(0, NZ)], sss.at[d])
            for i in range(3):
                arrived(senc, fws.at[d * 4 + i])

    @pl.loop(1, NX * NY)
    def _(i):
        arrived(far_own, far.at[i])
        arrived(far_own, fas.at[i])

    for i in range(NX):
        rows = far_all[i]
        for j in range(1, NY):
            rows = rows + far_all[j * NX + i]
        rows_out[:, i * RC:(i + 1) * RC] = rows
    rows = far_all[x]
    for j in range(1, NY):
        rows = rows + far_all[j * NX + x]
    rn_out[...] = jnp.where(k == 0, rows[:, 0:RB], rows[:, RB:RC]).reshape(RB)

    for i in range(NX):
        arrived(penc.at[row], sps.at[i])
        arrived(punit.at[row], sus.at[i])
    for i in range(1, NX):
        arrived(penc.at[row], pds.at[i])
        arrived(punit.at[row], pus.at[i])


NT = 256


def finish(u, rows, rn, cn, by_col, bh, bl, w_out, rn_out, cn_out, v_h, v_l, w_v, sem):
    puts = [pltpu.make_async_copy(rn, rn_out, sem.at[0]), pltpu.make_async_copy(cn, cn_out, sem.at[1])]
    for put in puts:
        put.start()
    by_row = 1.0 / jnp.sqrt(rows[...])
    row_mean = jnp.sum(rows[...], axis=1, keepdims=True) / R
    top = scale_alpha * jnp.sqrt(row_mean)
    v_h[...], v_l[...] = split(u[...] * by_row)
    by = by_col[:, 0:1] * top
    for n in range(DB // NT):
        cols = pl.ds(n * NT, NT)
        w = jnp.dot(v_h[...], bh[:, n * NT:(n + 1) * NT], preferred_element_type=f32)
        w += jnp.dot(v_l[...], bh[:, n * NT:(n + 1) * NT], preferred_element_type=f32)
        w += jnp.dot(v_h[...], bl[:, n * NT:(n + 1) * NT], preferred_element_type=f32)
        w_v[:, n * NT:(n + 1) * NT] = w * by
        put = pltpu.make_async_copy(w_v.at[:, cols], w_out.at[:, cols], sem.at[2 + n])
        put.start()
        puts.append(put)
    for put in puts:
        put.wait()


def per_device(activations, out_grads, basis, row_moment, col_moment):
    hbm = pl.BlockSpec(memory_space=pltpu.HBM)
    vmem = pl.BlockSpec(memory_space=pltpu.VMEM)
    dma = pltpu.SemaphoreType.DMA
    u, rows, rn, cn, by_col, bh, bl = pl.pallas_call(
        exchange,
        out_shape=(
            jax.ShapeDtypeStruct((FB, R), f32),
            jax.ShapeDtypeStruct((1, R), f32),
            jax.ShapeDtypeStruct((RB,), f32),
            jax.ShapeDtypeStruct((FB,), f32),
            jax.ShapeDtypeStruct((FB, 128), f32),
            jax.ShapeDtypeStruct((R, DB), bf16),
            jax.ShapeDtypeStruct((R, DB), bf16),
        ),
        in_specs=[hbm] * 5,
        out_specs=(vmem,) * 7,
        scratch_shapes=[
            pltpu.VMEM((TB, DB), bf16),
            pltpu.VMEM((DB, R), f32),
            pltpu.VMEM((RB,), f32),
            pltpu.VMEM((FB,), f32),
            pltpu.VMEM((ROWS, FH, TG), bf16),
            pltpu.VMEM((ROWS, RB, TB), bf16),
            pltpu.VMEM((ROWS, 1, TB), f32),
            pltpu.VMEM((ROWS, RB, TB), bf16),
            pltpu.VMEM((ROWS, 1, TB), f32),
            pltpu.VMEM((ROWS, SB, TB), bf16),
            pltpu.VMEM((ROWS, 1, TB), f32),
            pltpu.VMEM((RB, TB), bf16),
            pltpu.VMEM((SB, TB), bf16),
            pltpu.VMEM((2, 1, TB), f32),
            pltpu.VMEM((2, COLS, RB, TB), bf16),
            pltpu.VMEM((2, NY, NZ, 2, 1, TB), f32),
            pltpu.VMEM((2, NZ, RB, TB), bf16),
            pltpu.VMEM((ROWS, 2 * RC, TG), bf16),
            pltpu.VMEM((2, 2 * RC, TG), bf16),
            pltpu.VMEM((FH, 2 * RC), f32),
            pltpu.VMEM((FH, RC), bf16),
            pltpu.VMEM((1, RC), f32),
            pltpu.VMEM((FH, RC), bf16),
            pltpu.VMEM((1, RC), f32),
            pltpu.VMEM((ROWS, FH, RC), bf16),
            pltpu.VMEM((ROWS, 1, RC), f32),
            pltpu.VMEM((1, RC), f32),
            pltpu.VMEM((2 * NZ, 1, RC), f32),
            pltpu.VMEM((1, RC), f32),
            pltpu.VMEM((NX * NY, 1, RC), f32),
            dma((5,)),
            *[dma((ROWS,))] * 8,
            *[dma((COLS,))] * 4,
            dma((4 * NY,)), dma((NZ,)), dma((NZ,)), dma((NY,)), dma((NY,)),
            dma((2,)), dma((2,)), dma((2,)), dma((2,)), dma, dma,
            dma((NY,)), dma((NY,)),
            dma((2,)), dma((2,)), dma((2,)), dma((2,)),
            dma((NX,)), dma((NX,)), dma((NX,)), dma((NX,)),
            dma((NX,)), dma((NX,)), dma((NX,)), dma((NX,)),
            dma((2 * NZ,)), dma((2 * NZ,)),
            dma((NX * NY,)), dma((NX * NY,)),
            pltpu.SemaphoreType.REGULAR,
        ],
        compiler_params=pltpu.CompilerParams(
            collective_id=0, has_side_effects=True, vmem_limit_bytes=30 * 2**20
        ),
    )(*[pltpu.with_memory_space_constraint(v, pltpu.HBM) for v in (activations, out_grads.T, basis, row_moment, col_moment)])
    w, rn, cn = pl.pallas_call(
        finish,
        out_shape=(
            jax.ShapeDtypeStruct((FB, DB), f32),
            jax.ShapeDtypeStruct((RB,), f32),
            jax.ShapeDtypeStruct((FB,), f32),
        ),
        in_specs=[vmem] * 7,
        out_specs=(hbm,) * 3,
        scratch_shapes=[
            pltpu.VMEM((FB, R), bf16),
            pltpu.VMEM((FB, R), bf16),
            pltpu.VMEM((FB, DB), f32),
            dma((2 + DB // NT,)),
        ],
        compiler_params=pltpu.CompilerParams(vmem_limit_bytes=30 * 2**20),
    )(u, rows, rn, cn, by_col, bh, bl)
    return w.T, rn, cn


def solution(mesh):
    in_specs = (P("col", "row"), P("row", "col"), P("row", None), P("row"), P("col"))
    out_specs = (P("row", "col"), P("row"), P("col"))
    return jax.shard_map(
        per_device, mesh=mesh, in_specs=in_specs, out_specs=out_specs, check_vma=False
    )
```

```python
import jax
import jax.numpy as jnp
from jax import lax
from jax.experimental import pallas as pl
from jax.experimental.pallas import tpu as pltpu
from jax.sharding import PartitionSpec as P

F = 22016
R = 512
MESH = pl.DeviceIdType.MESH
f32 = jnp.float32
bf16 = jnp.bfloat16

beta_two = 0.8
scale_alpha = 0.25
epsilon = 1e-30

NX, NY, NZ = 4, 4, 8
ROWS = 2 * NX
COLS = NY * NZ
RB = R // ROWS
RC = 2 * RB
TB = 128
TG = 512
DB = 1024
FB = F // COLS
FH = 352
FO = 2 * FH - FB
SB = RB // NY
LIFT = 2.0 ** 7.875


def split(v):
    high = v.astype(bf16)
    return high, (v - high.astype(f32)).astype(bf16)


def encode(u):
    top = jnp.maximum(jnp.max(jnp.abs(u), axis=0, keepdims=True), 1e-30)
    w = u * (LIFT / top)
    w = w * w
    w = w * w
    w = w * w
    w = w * w
    return jnp.where(u < 0, -w, w).astype(bf16), top * (1.0 / LIFT)


def decode(code, unit):
    t = code.astype(f32)
    m = jnp.exp2(jnp.log2(jnp.abs(t)) * 0.0625)
    m = jnp.where(t == 0, 0.0, m)
    return jnp.where(t < 0, -m, m) * unit


def exchange(act, grads, basis, rm, cm, u_out, rows_out, rn_out, cn_out, by_col_out, bh_out, bl_out,
             a_v, b_v, rm_v, cm_v, g_v, sp, su, srecv, urecv, frecv, furecv, senc, fenc, unit_own,
             sall, uall, fall, shl, shf, acc, fpenc, fpunit, fprecv, fpurecv,
             penc, punit, near_own, near_all, far_own, far_all,
             ld, s1s, s1r, u1s, u1r, f1s, f1r, fu1s, fu1r, bds, bdr, fds, fdr, fws, uzs, uzr, uys, uyr,
             g1s, g2s, gr, gss, sss, ssr, fss, fsr, fps, fpr,
             pds, pdr, pus, pur, sps, spr, sus, sur, nes, ner, fas, far, ysem):
    row, col = lax.axis_index("row"), lax.axis_index("col")
    x, k = row // 2, row % 2
    y, z = col // NZ, col % NZ

    def at_x(o, core):
        return (lax.rem(x + o + NX, NX) * 2 + core, col)

    sibling = (x * 2 + 1 - k, col)
    opposite = lax.rem(x + 2, NX)
    here = y != opposite

    def send(src, dst, ssem, rsem, dev):
        pltpu.make_async_remote_copy(src_ref=src, dst_ref=dst, send_sem=ssem, recv_sem=rsem,
                                     device_id=dev, device_id_type=MESH).start()

    def arrived(ref, sem):
        pltpu.make_async_copy(ref, ref, sem).wait()

    def half(core):
        return grads.at[pl.ds(core * (FB - FH), FH)]

    DH = DB // 2
    first = [
        pltpu.make_async_copy(act, a_v, ld.at[0]),
        pltpu.make_async_copy(basis.at[pl.ds(0, DH)], b_v.at[pl.ds(0, DH)], ld.at[1]),
        pltpu.make_async_copy(basis.at[pl.ds(DH, DH)], b_v.at[pl.ds(DH, DH)], ld.at[2]),
    ]
    loads = [
        pltpu.make_async_copy(half(k), g_v.at[row], ld.at[3]),
        pltpu.make_async_copy(rm, rm_v, ld.at[4]),
        pltpu.make_async_copy(cm, cm_v, ld.at[5]),
    ]
    for load in first:
        load.start()

    barrier = pltpu.get_barrier_semaphore()
    for i in range(1, ROWS):
        pl.semaphore_signal(barrier, inc=1, device_id=(lax.rem(row + i, ROWS), col), device_id_type=MESH)
    for i in range(1, NZ):
        pl.semaphore_signal(barrier, inc=1, device_id=(row, y * NZ + lax.rem(z + i, NZ)), device_id_type=MESH)
    for i in range(1, NY):
        pl.semaphore_signal(barrier, inc=1, device_id=(row, lax.rem(y + i, NY) * NZ + z), device_id_type=MESH)
    @pl.when(y != x)
    def _():
        for r in range(ROWS):
            pl.semaphore_signal(barrier, inc=1, device_id=(r, x * NZ + z), device_id_type=MESH)

    first[0].wait()
    part = jnp.zeros((TB, R), f32)
    for h in range(2):
        first[1 + h].wait()
        high, low = split(b_v[h * DH:(h + 1) * DH, :])
        a = a_v[:, h * DH:(h + 1) * DH]
        part = part + jnp.dot(a, high, preferred_element_type=f32) + jnp.dot(a, low, preferred_element_type=f32)
    part = part.T
    for r in range(ROWS):
        code, unit = encode(part[r * RB:(r + 1) * RB])
        sp[r] = code
        su[r] = unit
    pl.semaphore_wait(barrier, ROWS + NZ + NY - 3 + 2 * (NY - 1))
    for i in range(1, NY):
        pl.semaphore_signal(ysem, inc=1, device_id=(row, lax.rem(y + i, NY) * NZ + z), device_id_type=MESH)
    for i in range(1, ROWS):
        peer = lax.rem(row + i, ROWS)

        @pl.when(peer // 2 != lax.rem(y + 2, NY))
        def _():
            send(sp.at[peer], srecv.at[row], s1s.at[i], s1r.at[i], (peer, col))
            send(su.at[peer], urecv.at[row], u1s.at[i], u1r.at[i], (peer, col))
    over = lax.rem(y + 2, NY) * 2
    for core in range(2):
        for j in range(NY):
            @pl.when((y * 2 + core != row) | (y != j))
            def _():
                dev = (y * 2 + core, j * NZ + z)
                send(sp.at[over + core, pl.ds(j * SB, SB)], frecv.at[row], f1s.at[core * NY + j], f1r.at[row], dev)
                send(su.at[over + core], furecv.at[row], fu1s.at[core * NY + j], fu1r.at[row], dev)
    for load in loads:
        load.start()

    pl.semaphore_wait(ysem, NY - 1)

    for core in range(2):
        send(half(core), g_v.at[row], g1s.at[core], gr.at[row], at_x(1, core))
        send(half(core), g_v.at[row], g2s.at[core], gr.at[row], at_x(-1, core))
    send(half(1 - k), g_v.at[row], gss, gr.at[row], sibling)

    @pl.when(y == x)
    def _():
        frecv[row] = sp[opposite * 2 + k, pl.ds(pl.multiple_of(y * SB, SB), SB)]
        furecv[row] = su[opposite * 2 + k]
    for r in range(ROWS):
        @pl.when((y != x) | (row != r))
        def _():
            arrived(frecv.at[row], f1r.at[r])
            arrived(furecv.at[row], fu1r.at[r])
    total = decode(frecv[0], furecv[0])
    for r in range(1, ROWS):
        total = total + decode(frecv[r], furecv[r])
    code, unit = encode(total)
    fenc[...] = code
    unit_own[1] = unit
    fall[k, z, pl.ds(pl.multiple_of(y * SB, SB), SB)] = code
    unit_own[0] = unit

    @pl.when(here)
    def _():
        srecv[row] = sp[row]
        urecv[row] = su[row]
        for i in range(1, ROWS):
            arrived(srecv.at[row], s1r.at[i])
            arrived(urecv.at[row], u1r.at[i])
        total = decode(srecv[0], urecv[0])
        for r in range(1, ROWS):
            total = total + decode(srecv[r], urecv[r])
        code, unit = encode(total)
        senc[...] = code
        unit_own[0] = unit
        sall[k, col] = code
    uall[k, y, z] = unit_own[...]
    for j in range(1, NZ):
        send(unit_own, uall.at[k, y, z], uzs.at[j], uzr.at[j], (row, y * NZ + lax.rem(z + j, NZ)))

    def spread(steps):
        @pl.when(here)
        def _():
            for j in steps:
                for d in (1, 2, 3, 0):
                    if j or d:
                        dev = (row, lax.rem(y + d, NY) * NZ + lax.rem(z + j, NZ))
                        send(senc, sall.at[k, col], bds.at[d * NZ + j], bdr.at[d * NZ + j], dev)

    spread((2, 6))
    for d in (1, 2, 3, 0):
        @pl.loop(0 if d else 1, NZ)
        def _(j):
            dev = (row, lax.rem(y + d, NY) * NZ + lax.rem(z + j, NZ))
            send(fenc, fall.at[k, z, pl.ds(pl.multiple_of(y * SB, SB), SB)], fds.at[d * NZ + j], fdr.at[d * NZ + j], dev)
    spread((1, 7, 0))

    turned_h, turned_l = split(b_v[...].T)
    bh_out[...] = turned_h
    bl_out[...] = turned_l

    def project(g, sides):
        return lax.dot_general(g, sides, (((1,), (1,)), ((), ())), preferred_element_type=f32)

    for j in range(1, NZ):
        arrived(unit_own, uzr.at[j])
    for d in range(1, NY):
        send(uall.at[k, y], uall.at[k, y], uys.at[d], uyr.at[d], (row, lax.rem(y + d, NY) * NZ + z))

    def hand_on(d, source, j, sem):
        b = lax.rem(y + NY - d, NY) * NZ + lax.rem(z + source, NZ)
        dev = (row, y * NZ + lax.rem(z + j, NZ))
        send(sall.at[k, b], sall.at[k, b], fws.at[d * 4 + sem], bdr.at[d * NZ + lax.rem(NZ - source + j, NZ)], dev)

    for d in (1, 2, 3, 0):
        @pl.when(lax.rem(y + NY - d, NY) != opposite)
        def _():
            arrived(senc, bdr.at[d * NZ + 2])
            hand_on(d, NZ - 2, 1, 0)
            arrived(senc, bdr.at[d * NZ + 6])
            hand_on(d, 2, NZ - 1, 1)

            @pl.when(z % 2 == 0)
            def _():
                hand_on(d, NZ - 2, 2, 2)

            @pl.when(z % 2 == 1)
            def _():
                hand_on(d, 2, NZ - 2, 2)

    for d in (1, 2, 3, 0):
        @pl.loop(0 if d else 1, NZ)
        def _(j):
            arrived(fenc, fdr.at[d * NZ + j])
    send(fall.at[k], fall.at[k], fss.at[0], fsr.at[0], sibling)
    for d in range(1, NY):
        arrived(uall.at[k, y], uyr.at[d])
    send(uall.at[k], uall.at[k], fss.at[1], fsr.at[1], sibling)
    arrived(g_v.at[row], gr.at[x * 2 + 1 - k])
    arrived(fall.at[k], fsr.at[0])
    arrived(uall.at[k], fsr.at[1])
    for b in range(NZ):
        r, at = b // 4, b % 4 * TB
        for core in range(2):
            units = jnp.concatenate([jnp.broadcast_to(uall[core, j, b, 1], (SB, TB)) for j in range(NY)], axis=0)
            high, low = split(decode(fall[core, b], units))
            shf[r, core * RB:(core + 1) * RB, at:at + TB] = high
            shf[r, RC + core * RB:RC + (core + 1) * RB, at:at + TB] = low
    for load in loads:
        load.wait()
    acc[...] = project(g_v[x * 2], shf[0])
    acc[...] += project(g_v[x * 2 + 1], shf[1])
    code, unit = encode(acc[:, 0:RC] + acc[:, RC:2 * RC])
    fpenc[...] = code
    fpunit[...] = unit
    send(fpenc, fprecv, fps.at[0], fpr.at[0], at_x(2, k))
    send(fpunit, fpurecv, fps.at[1], fpr.at[1], at_x(2, k))

    def share(d):
        first = lax.rem(y + NY - d, NY)

        @pl.when(first != opposite)
        def _():
            for j in (0, 1, 7, 3, 4, 5):
                if j or d:
                    arrived(senc, bdr.at[d * NZ + j])
            some = pl.ds(first * NZ, NZ)
            send(sall.at[k, some], sall.at[k, some], sss.at[d], ssr.at[d], sibling)

    def unpack(d):
        first = lax.rem(y + NY - d, NY)

        @pl.when(first != opposite)
        def _():
            some = pl.ds(first * NZ, NZ)
            arrived(sall.at[k, some], ssr.at[d])
            for j in range(NZ):
                b = first * NZ + j
                r = first * 2 + j // 4
                at = j % 4 * TB
                for core in range(2):
                    high, low = split(decode(sall[core, b], uall[core, first, j, 0]))
                    shl[r, core * RB:(core + 1) * RB, at:at + TB] = high
                    shl[r, RC + core * RB:RC + (core + 1) * RB, at:at + TB] = low

    def add(d):
        first = lax.rem(y + NY - d, NY)

        @pl.when(first != opposite)
        def _():
            @pl.when(first != x)
            def _():
                arrived(g_v.at[row], gr.at[first * 2])
                arrived(g_v.at[row], gr.at[first * 2 + 1])
            for i in range(2):
                acc[...] += project(g_v[first * 2 + i], shl[first * 2 + i])

    acc[...] = jnp.zeros_like(acc)
    share(1)
    share(2)
    unpack(1)
    share(3)
    unpack(2)
    add(1)
    share(0)
    unpack(3)
    add(2)
    unpack(0)
    add(3)
    add(0)
    arrived(fprecv, fpr.at[0])
    arrived(fpurecv, fpr.at[1])

    mine = acc[:, 0:RC] + acc[:, RC:2 * RC] + decode(fprecv[...], fpurecv[...])
    own = lax.broadcasted_iota(jnp.int32, (FH, RC), 0) >= FO * k
    sums = jnp.sum(jnp.where(own, mine * mine + epsilon, 0.0), axis=0, keepdims=True)
    old = rm_v[...].reshape(1, RB)
    old = jnp.concatenate([old, old], axis=1)
    lane = lax.broadcasted_iota(jnp.int32, (1, RC), 1)
    joins = (lane // RB == k) & (col == 0)
    near = (1.0 - beta_two) * (sums / F) + jnp.where(joins, beta_two * old, 0.0)
    near_own[...] = near
    near_at = k * NZ + z
    near_all[near_at] = near

    @pl.loop(1, 2 * NZ)
    def _(i):
        to = lax.rem(near_at + i, 2 * NZ)
        send(near_own, near_all.at[near_at], nes.at[i], ner.at[i], (x * 2 + to // NZ, y * NZ + lax.rem(to, NZ)))

    code, unit = encode(mine)
    penc[row] = code
    punit[row] = unit
    for i in (2, 1, 3):
        send(penc.at[row], penc.at[row], pds.at[i], pdr.at[i], at_x(i, k))
        send(punit.at[row], punit.at[row], pus.at[i], pur.at[i], at_x(i, k))
    send(penc.at[row], penc.at[row], sps.at[0], spr.at[0], sibling)
    send(punit.at[row], punit.at[row], sus.at[0], sur.at[0], sibling)

    @pl.loop(1, 2 * NZ)
    def _(i):
        arrived(near_own, ner.at[i])

    mid = jnp.sum(near_all[...], axis=0)
    far_own[...] = mid
    far_at = y * NX + x
    far_all[far_at] = mid

    @pl.loop(1, NX * NY)
    def _(i):
        to = lax.rem(far_at + i, NX * NY)
        send(far_own, far_all.at[far_at], fas.at[i], far.at[i], (lax.rem(to, NX) * 2 + k, to // NX * NZ + z))

    for i in (1, 3, 2):
        piece = lax.rem(x + NX - i, NX) * 2 + k
        arrived(penc.at[piece], pdr.at[i])
        send(penc.at[piece], penc.at[piece], sps.at[i], spr.at[i], sibling)
        arrived(punit.at[piece], pur.at[i])
        send(punit.at[piece], punit.at[piece], sus.at[i], sur.at[i], sibling)
    for i in range(NX):
        arrived(penc.at[row], spr.at[i])
        arrived(punit.at[row], sur.at[i])
    col_sum = [jnp.zeros((FH, 1), f32), jnp.zeros((FB - FH, 1), f32)]
    for r in range(ROWS):
        c = r % 2
        u = decode(penc[r], punit[r])[FO * c:]
        u_out[c * FH:c * FH + FH - FO * c, (r // 2) * RC:(r // 2 + 1) * RC] = u
        col_sum[c] += jnp.sum(u * u + epsilon, axis=1, keepdims=True)
    old = jnp.broadcast_to(cm_v[...].reshape(1, FB), (128, FB)).T
    col_next = beta_two * old + (1.0 - beta_two) * (jnp.concatenate(col_sum, axis=0) / R)
    cn_out[...] = col_next.T[0]
    by_col_out[...] = 1.0 / jnp.sqrt(col_next)

    for i in range(1, ROWS):
        @pl.when(lax.rem(row + i, ROWS) // 2 != lax.rem(y + 2, NY))
        def _():
            arrived(srecv.at[row], s1s.at[i])
            arrived(urecv.at[row], u1s.at[i])
    for core in range(2):
        for j in range(NY):
            @pl.when((y * 2 + core != row) | (y != j))
            def _():
                arrived(frecv.at[row], f1s.at[core * NY + j])
                arrived(furecv.at[row], fu1s.at[core * NY + j])

    @pl.loop(1, COLS)
    def _(i):
        arrived(fenc, fds.at[i])

    @pl.when(here)
    def _():
        for d in range(NY):
            for j in (0, 1, 2, 6, 7):
                if j or d:
                    arrived(senc, bds.at[d * NZ + j])
    for j in range(1, NZ):
        arrived(unit_own, uzs.at[j])
    for d in range(1, NY):
        arrived(uall.at[k, y], uys.at[d])

    @pl.loop(1, 2 * NZ)
    def _(i):
        arrived(near_own, nes.at[i])
    for i in range(2):
        arrived(g_v.at[row], g1s.at[i])
        arrived(g_v.at[row], g2s.at[i])
    arrived(g_v.at[row], gss)
    arrived(fall.at[k], fss.at[0])
    arrived(uall.at[k], fss.at[1])
    arrived(fpenc, fps.at[0])
    arrived(fpunit, fps.at[1])
    for d in range(NY):
        @pl.when(lax.rem(y + NY - d, NY) != opposite)
        def _():
            arrived(sall.at[k, pl.ds(0, NZ)], sss.at[d])
            for i in range(3):
                arrived(senc, fws.at[d * 4 + i])

    @pl.loop(1, NX * NY)
    def _(i):
        arrived(far_own, far.at[i])
        arrived(far_own, fas.at[i])

    for i in range(NX):
        rows = far_all[i]
        for j in range(1, NY):
            rows = rows + far_all[j * NX + i]
        rows_out[:, i * RC:(i + 1) * RC] = rows
    rows = far_all[x]
    for j in range(1, NY):
        rows = rows + far_all[j * NX + x]
    rn_out[...] = jnp.where(k == 0, rows[:, 0:RB], rows[:, RB:RC]).reshape(RB)

    for i in range(NX):
        arrived(penc.at[row], sps.at[i])
        arrived(punit.at[row], sus.at[i])
    for i in range(1, NX):
        arrived(penc.at[row], pds.at[i])
        arrived(punit.at[row], pus.at[i])


NT = 256


def finish(u, rows, rn, cn, by_col, bh, bl, w_out, rn_out, cn_out, v_h, v_l, w_v, sem):
    puts = [pltpu.make_async_copy(rn, rn_out, sem.at[0]), pltpu.make_async_copy(cn, cn_out, sem.at[1])]
    for put in puts:
        put.start()
    by_row = 1.0 / jnp.sqrt(rows[...])
    row_mean = jnp.sum(rows[...], axis=1, keepdims=True) / R
    top = scale_alpha * jnp.sqrt(row_mean)
    v_h[...], v_l[...] = split(u[...] * by_row)
    by = by_col[:, 0:1] * top
    for n in range(DB // NT):
        cols = pl.ds(n * NT, NT)
        w = jnp.dot(v_h[...], bh[:, n * NT:(n + 1) * NT], preferred_element_type=f32)
        w += jnp.dot(v_l[...], bh[:, n * NT:(n + 1) * NT], preferred_element_type=f32)
        w += jnp.dot(v_h[...], bl[:, n * NT:(n + 1) * NT], preferred_element_type=f32)
        w_v[:, n * NT:(n + 1) * NT] = w * by
        put = pltpu.make_async_copy(w_v.at[:, cols], w_out.at[:, cols], sem.at[2 + n])
        put.start()
        puts.append(put)
    for put in puts:
        put.wait()


def per_device(activations, out_grads, basis, row_moment, col_moment):
    hbm = pl.BlockSpec(memory_space=pltpu.HBM)
    vmem = pl.BlockSpec(memory_space=pltpu.VMEM)
    dma = pltpu.SemaphoreType.DMA
    u, rows, rn, cn, by_col, bh, bl = pl.pallas_call(
        exchange,
        out_shape=(
            jax.ShapeDtypeStruct((FB, R), f32),
            jax.ShapeDtypeStruct((1, R), f32),
            jax.ShapeDtypeStruct((RB,), f32),
            jax.ShapeDtypeStruct((FB,), f32),
            jax.ShapeDtypeStruct((FB, 128), f32),
            jax.ShapeDtypeStruct((R, DB), bf16),
            jax.ShapeDtypeStruct((R, DB), bf16),
        ),
        in_specs=[hbm] * 5,
        out_specs=(vmem,) * 7,
        scratch_shapes=[
            pltpu.VMEM((TB, DB), bf16),
            pltpu.VMEM((DB, R), f32),
            pltpu.VMEM((RB,), f32),
            pltpu.VMEM((FB,), f32),
            pltpu.VMEM((ROWS, FH, TG), bf16),
            pltpu.VMEM((ROWS, RB, TB), bf16),
            pltpu.VMEM((ROWS, 1, TB), f32),
            pltpu.VMEM((ROWS, RB, TB), bf16),
            pltpu.VMEM((ROWS, 1, TB), f32),
            pltpu.VMEM((ROWS, SB, TB), bf16),
            pltpu.VMEM((ROWS, 1, TB), f32),
            pltpu.VMEM((RB, TB), bf16),
            pltpu.VMEM((SB, TB), bf16),
            pltpu.VMEM((2, 1, TB), f32),
            pltpu.VMEM((2, COLS, RB, TB), bf16),
            pltpu.VMEM((2, NY, NZ, 2, 1, TB), f32),
            pltpu.VMEM((2, NZ, RB, TB), bf16),
            pltpu.VMEM((ROWS, 2 * RC, TG), bf16),
            pltpu.VMEM((2, 2 * RC, TG), bf16),
            pltpu.VMEM((FH, 2 * RC), f32),
            pltpu.VMEM((FH, RC), bf16),
            pltpu.VMEM((1, RC), f32),
            pltpu.VMEM((FH, RC), bf16),
            pltpu.VMEM((1, RC), f32),
            pltpu.VMEM((ROWS, FH, RC), bf16),
            pltpu.VMEM((ROWS, 1, RC), f32),
            pltpu.VMEM((1, RC), f32),
            pltpu.VMEM((2 * NZ, 1, RC), f32),
            pltpu.VMEM((1, RC), f32),
            pltpu.VMEM((NX * NY, 1, RC), f32),
            dma((6,)),
            *[dma((ROWS,))] * 8,
            *[dma((COLS,))] * 4,
            dma((4 * NY,)), dma((NZ,)), dma((NZ,)), dma((NY,)), dma((NY,)),
            dma((2,)), dma((2,)), dma((ROWS,)), dma,
            dma((NY,)), dma((NY,)),
            dma((2,)), dma((2,)), dma((2,)), dma((2,)),
            dma((NX,)), dma((NX,)), dma((NX,)), dma((NX,)),
            dma((NX,)), dma((NX,)), dma((NX,)), dma((NX,)),
            dma((2 * NZ,)), dma((2 * NZ,)),
            dma((NX * NY,)), dma((NX * NY,)),
            pltpu.SemaphoreType.REGULAR,
        ],
        compiler_params=pltpu.CompilerParams(
            collective_id=0, has_side_effects=True, vmem_limit_bytes=30 * 2**20
        ),
    )(*[pltpu.with_memory_space_constraint(v, pltpu.HBM) for v in (activations, out_grads.T, basis, row_moment, col_moment)])
    w, rn, cn = pl.pallas_call(
        finish,
        out_shape=(
            jax.ShapeDtypeStruct((FB, DB), f32),
            jax.ShapeDtypeStruct((RB,), f32),
            jax.ShapeDtypeStruct((FB,), f32),
        ),
        in_specs=[vmem] * 7,
        out_specs=(hbm,) * 3,
        scratch_shapes=[
            pltpu.VMEM((FB, R), bf16),
            pltpu.VMEM((FB, R), bf16),
            pltpu.VMEM((FB, DB), f32),
            dma((2 + DB // NT,)),
        ],
        compiler_params=pltpu.CompilerParams(vmem_limit_bytes=30 * 2**20),
    )(u, rows, rn, cn, by_col, bh, bl)
    return w.T, rn, cn


def solution(mesh):
    in_specs = (P("col", "row"), P("row", "col"), P("row", None), P("row"), P("col"))
    out_specs = (P("row", "col"), P("row"), P("col"))
    return jax.shard_map(
        per_device, mesh=mesh, in_specs=in_specs, out_specs=out_specs, check_vma=False
    )
```

```python
import jax
import jax.numpy as jnp
from jax import lax
from jax.experimental import pallas as pl
from jax.experimental.pallas import tpu as pltpu
from jax.sharding import PartitionSpec as P

F = 22016
R = 512
MESH = pl.DeviceIdType.MESH
f32 = jnp.float32
bf16 = jnp.bfloat16

beta_two = 0.8
scale_alpha = 0.25
epsilon = 1e-30

NX, NY, NZ = 4, 4, 8
ROWS = 2 * NX
COLS = NY * NZ
RB = R // ROWS
RC = 2 * RB
TB = 128
TG = 512
DB = 1024
FB = F // COLS
FH = 352
FO = 2 * FH - FB
SB = RB // NY
LIFT = 2.0 ** 7.875


def split(v):
    high = v.astype(bf16)
    return high, (v - high.astype(f32)).astype(bf16)


def encode(u):
    top = jnp.maximum(jnp.max(jnp.abs(u), axis=0, keepdims=True), 1e-30)
    w = u * (LIFT / top)
    w = w * w
    w = w * w
    w = w * w
    w = w * w
    return jnp.where(u < 0, -w, w).astype(bf16), top * (1.0 / LIFT)


def decode(code, unit):
    t = code.astype(f32)
    m = jnp.exp2(jnp.log2(jnp.abs(t)) * 0.0625)
    m = jnp.where(t == 0, 0.0, m)
    return jnp.where(t < 0, -m, m) * unit


def exchange(act, grads, basis, rm, cm, u_out, rows_out, rn_out, cn_out, by_col_out, bh_out, bl_out,
             a_v, b_v, rm_v, cm_v, g_v, sp, su, srecv, urecv, frecv, furecv, senc, fenc, unit_own,
             sall, uall, fall, shl, shf, acc, fpenc, fpunit, fprecv, fpurecv,
             penc, punit, near_own, near_all, far_own, far_all,
             ld, s1s, s1r, u1s, u1r, f1s, f1r, fu1s, fu1r, bds, bdr, fds, fdr, fws, uzs, uzr, uys, uyr,
             g1s, g2s, gr, gss, sss, ssr, fss, fsr, fps, fpr,
             pds, pdr, pus, pur, sps, spr, sus, sur, nes, ner, fas, far, ysem):
    row, col = lax.axis_index("row"), lax.axis_index("col")
    x, k = row // 2, row % 2
    y, z = col // NZ, col % NZ

    def at_x(o, core):
        return (lax.rem(x + o + NX, NX) * 2 + core, col)

    sibling = (x * 2 + 1 - k, col)
    opposite = lax.rem(x + 2, NX)
    here = y != opposite

    def send(src, dst, ssem, rsem, dev):
        pltpu.make_async_remote_copy(src_ref=src, dst_ref=dst, send_sem=ssem, recv_sem=rsem,
                                     device_id=dev, device_id_type=MESH).start()

    def arrived(ref, sem):
        pltpu.make_async_copy(ref, ref, sem).wait()

    def half(core):
        return grads.at[pl.ds(core * (FB - FH), FH)]

    DH = DB // 2
    first = [
        pltpu.make_async_copy(act, a_v, ld.at[0]),
        pltpu.make_async_copy(basis.at[pl.ds(0, DH)], b_v.at[pl.ds(0, DH)], ld.at[1]),
        pltpu.make_async_copy(basis.at[pl.ds(DH, DH)], b_v.at[pl.ds(DH, DH)], ld.at[2]),
    ]
    loads = [
        pltpu.make_async_copy(half(k), g_v.at[row], ld.at[3]),
        pltpu.make_async_copy(rm, rm_v, ld.at[4]),
        pltpu.make_async_copy(cm, cm_v, ld.at[5]),
    ]
    for load in first:
        load.start()

    barrier = pltpu.get_barrier_semaphore()
    for i in range(1, ROWS):
        pl.semaphore_signal(barrier, inc=1, device_id=(lax.rem(row + i, ROWS), col), device_id_type=MESH)
    for i in range(1, NZ):
        pl.semaphore_signal(barrier, inc=1, device_id=(row, y * NZ + lax.rem(z + i, NZ)), device_id_type=MESH)
    for i in range(1, NY):
        pl.semaphore_signal(barrier, inc=1, device_id=(row, lax.rem(y + i, NY) * NZ + z), device_id_type=MESH)
    @pl.when(y != x)
    def _():
        for r in range(ROWS):
            pl.semaphore_signal(barrier, inc=1, device_id=(r, x * NZ + z), device_id_type=MESH)

    first[0].wait()
    part = jnp.zeros((TB, R), f32)
    for h in range(2):
        first[1 + h].wait()
        high, low = split(b_v[h * DH:(h + 1) * DH, :])
        a = a_v[:, h * DH:(h + 1) * DH]
        part = part + jnp.dot(a, high, preferred_element_type=f32) + jnp.dot(a, low, preferred_element_type=f32)
    part = part.T
    for r in range(ROWS):
        code, unit = encode(part[r * RB:(r + 1) * RB])
        sp[r] = code
        su[r] = unit
    pl.semaphore_wait(barrier, ROWS + NZ + NY - 3 + 2 * (NY - 1))
    for i in range(1, NY):
        pl.semaphore_signal(ysem, inc=1, device_id=(row, lax.rem(y + i, NY) * NZ + z), device_id_type=MESH)
    over = lax.rem(y + 2, NY) * 2
    for core in range(2):
        for j in range(NY):
            @pl.when((y * 2 + core != row) | (y != j))
            def _():
                dev = (y * 2 + core, j * NZ + z)
                send(sp.at[over + core, pl.ds(j * SB, SB)], frecv.at[row], f1s.at[core * NY + j], f1r.at[row], dev)
                send(su.at[over + core], furecv.at[row], fu1s.at[core * NY + j], fu1r.at[row], dev)
    for i in range(1, ROWS):
        peer = lax.rem(row + i, ROWS)

        @pl.when(peer // 2 != lax.rem(y + 2, NY))
        def _():
            send(sp.at[peer], srecv.at[row], s1s.at[i], s1r.at[i], (peer, col))
            send(su.at[peer], urecv.at[row], u1s.at[i], u1r.at[i], (peer, col))

    for load in loads:
        load.start()

    pl.semaphore_wait(ysem, NY - 1)

    for core in range(2):
        send(half(core), g_v.at[row], g1s.at[core], gr.at[row], at_x(1, core))
        send(half(core), g_v.at[row], g2s.at[core], gr.at[row], at_x(-1, core))
    send(half(1 - k), g_v.at[row], gss, gr.at[row], sibling)

    @pl.when(y == x)
    def _():
        frecv[row] = sp[opposite * 2 + k, pl.ds(pl.multiple_of(y * SB, SB), SB)]
        furecv[row] = su[opposite * 2 + k]
    for r in range(ROWS):
        @pl.when((y != x) | (row != r))
        def _():
            arrived(frecv.at[row], f1r.at[r])
            arrived(furecv.at[row], fu1r.at[r])
    total = decode(frecv[0], furecv[0])
    for r in range(1, ROWS):
        total = total + decode(frecv[r], furecv[r])
    code, unit = encode(total)
    fenc[...] = code
    unit_own[1] = unit
    fall[k, z, pl.ds(pl.multiple_of(y * SB, SB), SB)] = code
    unit_own[0] = unit

    @pl.when(here)
    def _():
        srecv[row] = sp[row]
        urecv[row] = su[row]
        for i in range(1, ROWS):
            arrived(srecv.at[row], s1r.at[i])
            arrived(urecv.at[row], u1r.at[i])
        total = decode(srecv[0], urecv[0])
        for r in range(1, ROWS):
            total = total + decode(srecv[r], urecv[r])
        code, unit = encode(total)
        senc[...] = code
        unit_own[0] = unit
        sall[k, col] = code
    uall[k, y, z] = unit_own[...]
    for j in range(1, NZ):
        send(unit_own, uall.at[k, y, z], uzs.at[j], uzr.at[j], (row, y * NZ + lax.rem(z + j, NZ)))

    def spread(steps):
        @pl.when(here)
        def _():
            for j in steps:
                for d in (1, 2, 3, 0):
                    if j or d:
                        dev = (row, lax.rem(y + d, NY) * NZ + lax.rem(z + j, NZ))
                        send(senc, sall.at[k, col], bds.at[d * NZ + j], bdr.at[d * NZ + j], dev)

    spread((2, 6))
    for d in (1, 2, 3, 0):
        @pl.loop(0 if d else 1, NZ)
        def _(j):
            dev = (row, lax.rem(y + d, NY) * NZ + lax.rem(z + j, NZ))
            send(fenc, fall.at[k, z, pl.ds(pl.multiple_of(y * SB, SB), SB)], fds.at[d * NZ + j], fdr.at[d * NZ + j], dev)
    spread((1, 7, 0))

    turned_h, turned_l = split(b_v[...].T)
    bh_out[...] = turned_h
    bl_out[...] = turned_l

    def project(g, sides):
        return lax.dot_general(g, sides, (((1,), (1,)), ((), ())), preferred_element_type=f32)

    for j in range(1, NZ):
        arrived(unit_own, uzr.at[j])
    for d in range(1, NY):
        send(uall.at[k, y], uall.at[k, y], uys.at[d], uyr.at[d], (row, lax.rem(y + d, NY) * NZ + z))

    def hand_on(d, source, j, sem):
        b = lax.rem(y + NY - d, NY) * NZ + lax.rem(z + source, NZ)
        dev = (row, y * NZ + lax.rem(z + j, NZ))
        send(sall.at[k, b], sall.at[k, b], fws.at[d * 4 + sem], bdr.at[d * NZ + lax.rem(NZ - source + j, NZ)], dev)

    for d in (1, 2, 3, 0):
        @pl.when(lax.rem(y + NY - d, NY) != opposite)
        def _():
            arrived(senc, bdr.at[d * NZ + 2])
            hand_on(d, NZ - 2, 1, 0)
            arrived(senc, bdr.at[d * NZ + 6])
            hand_on(d, 2, NZ - 1, 1)

            @pl.when(z % 2 == 0)
            def _():
                hand_on(d, NZ - 2, 2, 2)

            @pl.when(z % 2 == 1)
            def _():
                hand_on(d, 2, NZ - 2, 2)

    for d in (1, 2, 3, 0):
        @pl.loop(0 if d else 1, NZ)
        def _(j):
            arrived(fenc, fdr.at[d * NZ + j])
    send(fall.at[k], fall.at[k], fss.at[0], fsr.at[0], sibling)
    for d in range(1, NY):
        arrived(uall.at[k, y], uyr.at[d])
    send(uall.at[k], uall.at[k], fss.at[1], fsr.at[1], sibling)
    arrived(g_v.at[row], gr.at[x * 2 + 1 - k])
    arrived(fall.at[k], fsr.at[0])
    arrived(uall.at[k], fsr.at[1])
    for b in range(NZ):
        r, at = b // 4, b % 4 * TB
        for core in range(2):
            units = jnp.concatenate([jnp.broadcast_to(uall[core, j, b, 1], (SB, TB)) for j in range(NY)], axis=0)
            high, low = split(decode(fall[core, b], units))
            shf[r, core * RB:(core + 1) * RB, at:at + TB] = high
            shf[r, RC + core * RB:RC + (core + 1) * RB, at:at + TB] = low
    for load in loads:
        load.wait()
    acc[...] = project(g_v[x * 2], shf[0])
    acc[...] += project(g_v[x * 2 + 1], shf[1])
    code, unit = encode(acc[:, 0:RC] + acc[:, RC:2 * RC])
    fpenc[...] = code
    fpunit[...] = unit
    send(fpenc, fprecv, fps.at[0], fpr.at[0], at_x(2, k))
    send(fpunit, fpurecv, fps.at[1], fpr.at[1], at_x(2, k))

    def share(d):
        first = lax.rem(y + NY - d, NY)

        @pl.when(first != opposite)
        def _():
            for j in (0, 1, 7, 3, 4, 5):
                if j or d:
                    arrived(senc, bdr.at[d * NZ + j])
            some = pl.ds(first * NZ, NZ)
            send(sall.at[k, some], sall.at[k, some], sss.at[d], ssr.at[d], sibling)

    def unpack(d):
        first = lax.rem(y + NY - d, NY)

        @pl.when(first != opposite)
        def _():
            some = pl.ds(first * NZ, NZ)
            arrived(sall.at[k, some], ssr.at[d])
            for j in range(NZ):
                b = first * NZ + j
                r = first * 2 + j // 4
                at = j % 4 * TB
                for core in range(2):
                    high, low = split(decode(sall[core, b], uall[core, first, j, 0]))
                    shl[r, core * RB:(core + 1) * RB, at:at + TB] = high
                    shl[r, RC + core * RB:RC + (core + 1) * RB, at:at + TB] = low

    def add(d):
        first = lax.rem(y + NY - d, NY)

        @pl.when(first != opposite)
        def _():
            @pl.when(first != x)
            def _():
                arrived(g_v.at[row], gr.at[first * 2])
                arrived(g_v.at[row], gr.at[first * 2 + 1])
            for i in range(2):
                acc[...] += project(g_v[first * 2 + i], shl[first * 2 + i])

    acc[...] = jnp.zeros_like(acc)
    share(1)
    share(2)
    unpack(1)
    share(3)
    unpack(2)
    add(1)
    share(0)
    unpack(3)
    add(2)
    unpack(0)
    add(3)
    add(0)
    arrived(fprecv, fpr.at[0])
    arrived(fpurecv, fpr.at[1])

    mine = acc[:, 0:RC] + acc[:, RC:2 * RC] + decode(fprecv[...], fpurecv[...])
    own = lax.broadcasted_iota(jnp.int32, (FH, RC), 0) >= FO * k
    sums = jnp.sum(jnp.where(own, mine * mine + epsilon, 0.0), axis=0, keepdims=True)
    old = rm_v[...].reshape(1, RB)
    old = jnp.concatenate([old, old], axis=1)
    lane = lax.broadcasted_iota(jnp.int32, (1, RC), 1)
    joins = (lane // RB == k) & (col == 0)
    near = (1.0 - beta_two) * (sums / F) + jnp.where(joins, beta_two * old, 0.0)
    near_own[...] = near
    near_at = k * NZ + z
    near_all[near_at] = near

    @pl.loop(1, 2 * NZ)
    def _(i):
        to = lax.rem(near_at + i, 2 * NZ)
        send(near_own, near_all.at[near_at], nes.at[i], ner.at[i], (x * 2 + to // NZ, y * NZ + lax.rem(to, NZ)))

    code, unit = encode(mine)
    penc[row] = code
    punit[row] = unit
    for i in (2, 1, 3):
        send(penc.at[row], penc.at[row], pds.at[i], pdr.at[i], at_x(i, k))
        send(punit.at[row], punit.at[row], pus.at[i], pur.at[i], at_x(i, k))
    send(penc.at[row], penc.at[row], sps.at[0], spr.at[0], sibling)
    send(punit.at[row], punit.at[row], sus.at[0], sur.at[0], sibling)

    @pl.loop(1, 2 * NZ)
    def _(i):
        arrived(near_own, ner.at[i])

    mid = jnp.sum(near_all[...], axis=0)
    far_own[...] = mid
    far_at = y * NX + x
    far_all[far_at] = mid

    @pl.loop(1, NX * NY)
    def _(i):
        to = lax.rem(far_at + i, NX * NY)
        send(far_own, far_all.at[far_at], fas.at[i], far.at[i], (lax.rem(to, NX) * 2 + k, to // NX * NZ + z))

    for i in (1, 3, 2):
        piece = lax.rem(x + NX - i, NX) * 2 + k
        arrived(penc.at[piece], pdr.at[i])
        send(penc.at[piece], penc.at[piece], sps.at[i], spr.at[i], sibling)
        arrived(punit.at[piece], pur.at[i])
        send(punit.at[piece], punit.at[piece], sus.at[i], sur.at[i], sibling)
    for i in range(NX):
        arrived(penc.at[row], spr.at[i])
        arrived(punit.at[row], sur.at[i])
    col_sum = [jnp.zeros((FH, 1), f32), jnp.zeros((FB - FH, 1), f32)]
    for r in range(ROWS):
        c = r % 2
        u = decode(penc[r], punit[r])[FO * c:]
        u_out[c * FH:c * FH + FH - FO * c, (r // 2) * RC:(r // 2 + 1) * RC] = u
        col_sum[c] += jnp.sum(u * u + epsilon, axis=1, keepdims=True)
    old = jnp.broadcast_to(cm_v[...].reshape(1, FB), (128, FB)).T
    col_next = beta_two * old + (1.0 - beta_two) * (jnp.concatenate(col_sum, axis=0) / R)
    cn_out[...] = col_next.T[0]
    by_col_out[...] = 1.0 / jnp.sqrt(col_next)

    for i in range(1, ROWS):
        @pl.when(lax.rem(row + i, ROWS) // 2 != lax.rem(y + 2, NY))
        def _():
            arrived(srecv.at[row], s1s.at[i])
            arrived(urecv.at[row], u1s.at[i])
    for core in range(2):
        for j in range(NY):
            @pl.when((y * 2 + core != row) | (y != j))
            def _():
                arrived(frecv.at[row], f1s.at[core * NY + j])
                arrived(furecv.at[row], fu1s.at[core * NY + j])

    @pl.loop(1, COLS)
    def _(i):
        arrived(fenc, fds.at[i])

    @pl.when(here)
    def _():
        for d in range(NY):
            for j in (0, 1, 2, 6, 7):
                if j or d:
                    arrived(senc, bds.at[d * NZ + j])
    for j in range(1, NZ):
        arrived(unit_own, uzs.at[j])
    for d in range(1, NY):
        arrived(uall.at[k, y], uys.at[d])

    @pl.loop(1, 2 * NZ)
    def _(i):
        arrived(near_own, nes.at[i])
    for i in range(2):
        arrived(g_v.at[row], g1s.at[i])
        arrived(g_v.at[row], g2s.at[i])
    arrived(g_v.at[row], gss)
    arrived(fall.at[k], fss.at[0])
    arrived(uall.at[k], fss.at[1])
    arrived(fpenc, fps.at[0])
    arrived(fpunit, fps.at[1])
    for d in range(NY):
        @pl.when(lax.rem(y + NY - d, NY) != opposite)
        def _():
            arrived(sall.at[k, pl.ds(0, NZ)], sss.at[d])
            for i in range(3):
                arrived(senc, fws.at[d * 4 + i])

    @pl.loop(1, NX * NY)
    def _(i):
        arrived(far_own, far.at[i])
        arrived(far_own, fas.at[i])

    for i in range(NX):
        rows = far_all[i]
        for j in range(1, NY):
            rows = rows + far_all[j * NX + i]
        rows_out[:, i * RC:(i + 1) * RC] = rows
    rows = far_all[x]
    for j in range(1, NY):
        rows = rows + far_all[j * NX + x]
    rn_out[...] = jnp.where(k == 0, rows[:, 0:RB], rows[:, RB:RC]).reshape(RB)

    for i in range(NX):
        arrived(penc.at[row], sps.at[i])
        arrived(punit.at[row], sus.at[i])
    for i in range(1, NX):
        arrived(penc.at[row], pds.at[i])
        arrived(punit.at[row], pus.at[i])


NT = 256


def finish(u, rows, rn, cn, by_col, bh, bl, w_out, rn_out, cn_out, v_h, v_l, w_v, sem):
    puts = [pltpu.make_async_copy(rn, rn_out, sem.at[0]), pltpu.make_async_copy(cn, cn_out, sem.at[1])]
    for put in puts:
        put.start()
    by_row = 1.0 / jnp.sqrt(rows[...])
    row_mean = jnp.sum(rows[...], axis=1, keepdims=True) / R
    top = scale_alpha * jnp.sqrt(row_mean)
    v_h[...], v_l[...] = split(u[...] * by_row)
    by = by_col[:, 0:1] * top
    for n in range(DB // NT):
        cols = pl.ds(n * NT, NT)
        w = jnp.dot(v_h[...], bh[:, n * NT:(n + 1) * NT], preferred_element_type=f32)
        w += jnp.dot(v_l[...], bh[:, n * NT:(n + 1) * NT], preferred_element_type=f32)
        w += jnp.dot(v_h[...], bl[:, n * NT:(n + 1) * NT], preferred_element_type=f32)
        w_v[:, n * NT:(n + 1) * NT] = w * by
        put = pltpu.make_async_copy(w_v.at[:, cols], w_out.at[:, cols], sem.at[2 + n])
        put.start()
        puts.append(put)
    for put in puts:
        put.wait()


def per_device(activations, out_grads, basis, row_moment, col_moment):
    hbm = pl.BlockSpec(memory_space=pltpu.HBM)
    vmem = pl.BlockSpec(memory_space=pltpu.VMEM)
    dma = pltpu.SemaphoreType.DMA
    u, rows, rn, cn, by_col, bh, bl = pl.pallas_call(
        exchange,
        out_shape=(
            jax.ShapeDtypeStruct((FB, R), f32),
            jax.ShapeDtypeStruct((1, R), f32),
            jax.ShapeDtypeStruct((RB,), f32),
            jax.ShapeDtypeStruct((FB,), f32),
            jax.ShapeDtypeStruct((FB, 128), f32),
            jax.ShapeDtypeStruct((R, DB), bf16),
            jax.ShapeDtypeStruct((R, DB), bf16),
        ),
        in_specs=[hbm] * 5,
        out_specs=(vmem,) * 7,
        scratch_shapes=[
            pltpu.VMEM((TB, DB), bf16),
            pltpu.VMEM((DB, R), f32),
            pltpu.VMEM((RB,), f32),
            pltpu.VMEM((FB,), f32),
            pltpu.VMEM((ROWS, FH, TG), bf16),
            pltpu.VMEM((ROWS, RB, TB), bf16),
            pltpu.VMEM((ROWS, 1, TB), f32),
            pltpu.VMEM((ROWS, RB, TB), bf16),
            pltpu.VMEM((ROWS, 1, TB), f32),
            pltpu.VMEM((ROWS, SB, TB), bf16),
            pltpu.VMEM((ROWS, 1, TB), f32),
            pltpu.VMEM((RB, TB), bf16),
            pltpu.VMEM((SB, TB), bf16),
            pltpu.VMEM((2, 1, TB), f32),
            pltpu.VMEM((2, COLS, RB, TB), bf16),
            pltpu.VMEM((2, NY, NZ, 2, 1, TB), f32),
            pltpu.VMEM((2, NZ, RB, TB), bf16),
            pltpu.VMEM((ROWS, 2 * RC, TG), bf16),
            pltpu.VMEM((2, 2 * RC, TG), bf16),
            pltpu.VMEM((FH, 2 * RC), f32),
            pltpu.VMEM((FH, RC), bf16),
            pltpu.VMEM((1, RC), f32),
            pltpu.VMEM((FH, RC), bf16),
            pltpu.VMEM((1, RC), f32),
            pltpu.VMEM((ROWS, FH, RC), bf16),
            pltpu.VMEM((ROWS, 1, RC), f32),
            pltpu.VMEM((1, RC), f32),
            pltpu.VMEM((2 * NZ, 1, RC), f32),
            pltpu.VMEM((1, RC), f32),
            pltpu.VMEM((NX * NY, 1, RC), f32),
            dma((6,)),
            *[dma((ROWS,))] * 8,
            *[dma((COLS,))] * 4,
            dma((4 * NY,)), dma((NZ,)), dma((NZ,)), dma((NY,)), dma((NY,)),
            dma((2,)), dma((2,)), dma((ROWS,)), dma,
            dma((NY,)), dma((NY,)),
            dma((2,)), dma((2,)), dma((2,)), dma((2,)),
            dma((NX,)), dma((NX,)), dma((NX,)), dma((NX,)),
            dma((NX,)), dma((NX,)), dma((NX,)), dma((NX,)),
            dma((2 * NZ,)), dma((2 * NZ,)),
            dma((NX * NY,)), dma((NX * NY,)),
            pltpu.SemaphoreType.REGULAR,
        ],
        compiler_params=pltpu.CompilerParams(
            collective_id=0, has_side_effects=True, vmem_limit_bytes=30 * 2**20
        ),
    )(*[pltpu.with_memory_space_constraint(v, pltpu.HBM) for v in (activations, out_grads.T, basis, row_moment, col_moment)])
    w, rn, cn = pl.pallas_call(
        finish,
        out_shape=(
            jax.ShapeDtypeStruct((FB, DB), f32),
            jax.ShapeDtypeStruct((RB,), f32),
            jax.ShapeDtypeStruct((FB,), f32),
        ),
        in_specs=[vmem] * 7,
        out_specs=(hbm,) * 3,
        scratch_shapes=[
            pltpu.VMEM((FB, R), bf16),
            pltpu.VMEM((FB, R), bf16),
            pltpu.VMEM((FB, DB), f32),
            dma((2 + DB // NT,)),
        ],
        compiler_params=pltpu.CompilerParams(vmem_limit_bytes=30 * 2**20),
    )(u, rows, rn, cn, by_col, bh, bl)
    return w.T, rn, cn


def solution(mesh):
    in_specs = (P("col", "row"), P("row", "col"), P("row", None), P("row"), P("col"))
    out_specs = (P("row", "col"), P("row"), P("col"))
    return jax.shard_map(
        per_device, mesh=mesh, in_specs=in_specs, out_specs=out_specs, check_vma=False
    )
```
